256 devices in a mesh: ctx: 128 (over y, x, z), head: 2 (over core).
Axes of the slice: x: 4, y: 4, z: 8, core: 2. Of those that a mesh axis runs over, the one named last changes fastest.
Arguments:
- queries: bfloat16 [65536, 4, 4, 128], P('ctx', 'head')
- keys: bfloat16 [65536, 4, 128], P('ctx')
- values: bfloat16 [65536, 4, 128], P('ctx'), may hold values from -6 to 6
- output_gradient: bfloat16 [65536, 4, 4, 128], P('ctx', 'head'), may hold values from -6 to 6
- selected: int32 [128, 2], replicated, may hold values from 0 to 126, as said below
Outputs:
- attn_out: bfloat16 [65536, 4, 4, 128], P('ctx', 'head')
- grad_q: bfloat16 [65536, 4, 4, 128], P('ctx', 'head')
- grad_k: bfloat16 [65536, 4, 128], P('ctx', 'head')
- grad_v: bfloat16 [65536, 4, 128], P('ctx', 'head')
The draws below stay inside these ranges and needn't reach their ends.
Inputs may be any that keep to these rules, and one draw needn't show every extreme that they name: selected[b, j] <= b for every block b; an entry equal to b selects no block; for b >= 2 the two entries of a row differ and both are below b.
All inputs are finite; a program needn't handle non-finite values.
Results may differ from the reference program's by a relative error of at most 0.011.
Values may be sent and summed in bfloat16 or wider, within the bound.
No kernel may reach another device: no remote copies, remote signals or barrier semaphores. Data moves between devices by JAX's collectives and lax.ppermute only.
A program may use at most 128 MiB of HBM per device.

```python
import jax
import jax.numpy as jnp
from jax import lax

KEY_VALUE_HEADS = 4
QUERY_PER_KEY = 4
HEAD_DIMENSION = 128
BLK = 512
NB = 128
SEQUENCE_TOKENS = 65536


def draw_keys(key, part):
    return jnp.clip(jax.random.normal(jax.random.fold_in(key, 11), (SEQUENCE_TOKENS, KEY_VALUE_HEADS, HEAD_DIMENSION), jnp.float32), -6.0, 6.0).astype(jnp.bfloat16)


def draw_queries(key, part):
    return jnp.clip(jax.random.normal(jax.random.fold_in(key, 12), (SEQUENCE_TOKENS, QUERY_PER_KEY, KEY_VALUE_HEADS, HEAD_DIMENSION), jnp.float32), -6.0, 6.0).astype(jnp.bfloat16)


def draw_selected(key, part):
    index = jnp.arange(NB, dtype=jnp.int32)
    hottest = jax.random.randint(jax.random.fold_in(key, 1), (), 0, NB // 4)
    coin_flip = jax.random.randint(jax.random.fold_in(key, 2), (NB,), 0, 2)
    first_pick = jax.random.randint(jax.random.fold_in(key, 3), (NB,), 0, jnp.maximum(index, 1))
    first_pick = jnp.where((coin_flip == 1) & (index > hottest), hottest, first_pick)
    other_pick = jax.random.randint(jax.random.fold_in(key, 4), (NB,), 0, jnp.maximum(index - 1, 1))
    second_pick = other_pick + (other_pick >= first_pick).astype(jnp.int32)
    second_pick = jnp.where(index == 0, 0, second_pick)
    first_pick = jnp.where(index == NB - 1, hottest, first_pick)
    second_pick = jnp.where(index == NB - 1, NB - 2, second_pick)
    return jnp.stack([first_pick, second_pick], axis=1).astype(jnp.int32)


def steps_of(rng, dims, shards, low, high):
    def one(axis_at, parts):
        heights = jax.random.uniform(jax.random.fold_in(jax.random.fold_in(rng, 6), axis_at), (parts,), jnp.float32, low / len(shards), high / len(shards))
        return jnp.repeat(jnp.exp(heights), dims[axis_at] // parts).reshape((-1,) + (1,) * (len(dims) - axis_at - 1))

    factor_of = one(*shards[0])
    for cut in shards[1:]:
        factor_of = factor_of * one(*cut)
    return factor_of


def normal_values(own_key, dims, deviation, limit, cuts=(), kind=jnp.bfloat16):
    drawn = jax.random.normal(own_key, dims, jnp.float32) * deviation
    if len(cuts) > 0:
        drawn = steps_of(own_key, dims, cuts, -0.22, 0.18) * drawn
    return jnp.clip(drawn, min=-limit, max=limit).astype(kind)


def setup_inputs(seed: int = 0) -> dict:
    streams_of = jax.random.split(jax.random.key(seed), 6)
    return {
        "queries": draw_queries(jax.random.fold_in(streams_of[5], 71), 0),
        "keys": draw_keys(jax.random.fold_in(streams_of[5], 71), 0),
        "values": normal_values(streams_of[2], (SEQUENCE_TOKENS, KEY_VALUE_HEADS, HEAD_DIMENSION), 1.0, 6.0, ((0, 128),)),
        "output_gradient": normal_values(streams_of[3], (SEQUENCE_TOKENS, QUERY_PER_KEY, KEY_VALUE_HEADS, HEAD_DIMENSION), 1.0, 6.0, ((0, 128), (1, 2))),
        "selected": draw_selected(jax.random.fold_in(streams_of[5], 71), 0),
    }


def attend_block(block_q, block_k, block_v, block_g, visible, softmax_scale):
    query_f = block_q.astype(jnp.float32)
    key_f = block_k.astype(jnp.float32)
    value_f = block_v.astype(jnp.float32)
    grad_f = block_g.astype(jnp.float32)
    scores = jnp.einsum("qgnd,knd->gnqk", query_f, key_f) * softmax_scale
    scores = jnp.where(visible, scores, -jnp.inf)
    row_max = jnp.max(scores, axis=-1, keepdims=True)
    weights = jnp.exp(scores - row_max)
    probs = weights / jnp.sum(weights, axis=-1, keepdims=True)
    probs_low = probs.astype(jnp.bfloat16)
    block_out = jnp.einsum("gnqk,knd->qgnd", probs_low.astype(jnp.float32), value_f).astype(jnp.bfloat16)
    row_dot = jnp.sum(grad_f * block_out.astype(jnp.float32), axis=-1)
    grad_probs = jnp.einsum("qgnd,knd->gnqk", grad_f, value_f)
    grad_scores = (probs * (grad_probs - jnp.transpose(row_dot, (1, 2, 0))[..., None]) * softmax_scale).astype(jnp.bfloat16)
    block_dq = jnp.einsum("gnqk,knd->qgnd", grad_scores.astype(jnp.float32), key_f).astype(jnp.bfloat16)
    part_k = jnp.einsum("gnqk,qgnd->knd", grad_scores.astype(jnp.float32), query_f)
    part_v = jnp.einsum("gnqk,qgnd->knd", probs_low.astype(jnp.float32), grad_f)
    return block_out, block_dq, part_k, part_v


def reference(queries, keys, values, output_gradient, selected):
    softmax_scale = HEAD_DIMENSION ** -0.5
    position = jnp.arange(BLK, dtype=jnp.int32)
    causal = position[:, None] >= position[None, :]

    def block_rows(source, block_id):
        return lax.dynamic_slice_in_dim(source, (block_id * BLK).astype(jnp.int32), BLK, 0)

    def one_block(totals, block_id):
        grad_keys, grad_values = totals
        first_pick = selected[block_id, 0]
        second_pick = selected[block_id, 1]
        chosen_blocks = [first_pick, second_pick, block_id]
        block_k = jnp.concatenate([block_rows(keys, chosen) for chosen in chosen_blocks], axis=0)
        block_v = jnp.concatenate([block_rows(values, chosen) for chosen in chosen_blocks], axis=0)
        visible = jnp.concatenate([jnp.broadcast_to(first_pick < block_id, (BLK, BLK)), jnp.broadcast_to(second_pick < block_id, (BLK, BLK)), causal], axis=1)
        block_out, block_dq, part_k, part_v = attend_block(block_rows(queries, block_id), block_k, block_v, block_rows(output_gradient, block_id), visible, softmax_scale)
        for column, chosen in enumerate(chosen_blocks):
            start_row = (chosen * BLK).astype(jnp.int32)
            grad_keys = lax.dynamic_update_slice_in_dim(grad_keys, block_rows(grad_keys, chosen) + part_k[column * BLK:(column + 1) * BLK], start_row, 0)
            grad_values = lax.dynamic_update_slice_in_dim(grad_values, block_rows(grad_values, chosen) + part_v[column * BLK:(column + 1) * BLK], start_row, 0)
        return (grad_keys, grad_values), (block_out, block_dq)

    empty_grads = jnp.zeros(keys.shape, jnp.float32)
    (grad_keys, grad_values), (all_out, all_dq) = lax.scan(one_block, (empty_grads, empty_grads), jnp.arange(NB, dtype=jnp.int32))
    return (all_out.reshape(queries.shape), all_dq.reshape(queries.shape), grad_keys.astype(jnp.bfloat16), grad_values.astype(jnp.bfloat16))
```

```python
import functools
import math

import jax
import jax.numpy as jnp
from jax import lax
from jax.experimental import pallas as pl
from jax.experimental.pallas import tpu as pltpu
from jax.sharding import PartitionSpec as P

F32 = jnp.float32
BF16 = jnp.bfloat16
MIB = 1024 * 1024


def dot_nn(a, b):
    return lax.dot_general(a, b, (((1,), (0,)), ((), ())), preferred_element_type=F32)


def dot_nt(a, b):
    return lax.dot_general(a, b, (((1,), (1,)), ((), ())), preferred_element_type=F32)


def dot_tn(a, b):
    return lax.dot_general(a, b, (((0,), (0,)), ((), ())), preferred_element_type=F32)


def pick_kernel(picks, held, out):
    blocks, rows, _ = held.shape

    def body(step, _):
        for sub in range(8):
            at = step * 8 + sub
            for j in range(2):
                out[at, j * rows : (j + 1) * rows, :] = held[picks[at * 2 + j]]
        return 0

    lax.fori_loop(0, blocks // 8, body, 0)


def pick_pieces(held, picks):
    blocks, rows, width = held.shape
    return pl.pallas_call(
        pick_kernel,
        out_shape=jax.ShapeDtypeStruct((blocks, 2 * rows, width), held.dtype),
        in_specs=[
            pl.BlockSpec(memory_space=pltpu.SMEM),
            pl.BlockSpec(memory_space=pltpu.VMEM),
        ],
        out_specs=pl.BlockSpec(memory_space=pltpu.VMEM),
        name="pick_pieces",
    )(picks, held)


def collect_kernel(picks, arrived, out, total):
    blocks, rows2, _ = arrived.shape
    rows = rows2 // 2
    total[...] = jnp.zeros_like(total)

    def body(step, _):
        for sub in range(8):
            at = step * 8 + sub
            for j in range(2):
                owner = picks[at * 2 + j]
                total[owner] += arrived[at, j * rows : (j + 1) * rows, :].astype(F32)
        return 0

    lax.fori_loop(0, blocks // 8, body, 0)
    out[...] = total[...].astype(out.dtype)


def collect_pieces(arrived, picks):
    blocks, rows2, width = arrived.shape
    return pl.pallas_call(
        collect_kernel,
        out_shape=jax.ShapeDtypeStruct((blocks, rows2 // 2, width), arrived.dtype),
        in_specs=[
            pl.BlockSpec(memory_space=pltpu.SMEM),
            pl.BlockSpec(memory_space=pltpu.VMEM),
        ],
        out_specs=pl.BlockSpec(memory_space=pltpu.VMEM),
        scratch_shapes=[pltpu.VMEM((blocks, rows2 // 2, width), F32)],
        name="collect_pieces",
    )(picks, arrived)


def lower_triangle(rows):
    return lax.broadcasted_iota(jnp.int32, (rows, rows), 0) >= lax.broadcasted_iota(
        jnp.int32, (rows, rows), 1
    )


def own_forward_kernel(log_scale, q_ref, kv_ref, out_ref, lse_ref):
    half = q_ref.shape[2] // 2
    seen = lower_triangle(half)
    for tile in range(2):
        rows = slice(tile * half, (tile + 1) * half)
        query = q_ref[0, 0, rows, :]
        parts = []
        for col in range(tile + 1):
            cols = slice(col * half, (col + 1) * half)
            scores = dot_nt(query, kv_ref[0, 0, cols, :])
            if col == tile:
                scores = jnp.where(seen, scores, -jnp.inf)
            parts.append(scores)
        top = parts[0].max(axis=-1, keepdims=True)
        for scores in parts[1:]:
            top = jnp.maximum(top, scores.max(axis=-1, keepdims=True))
        top = top * log_scale
        weight, total = None, None
        for col, scores in enumerate(parts):
            cols = slice(col * half, (col + 1) * half)
            probs = jnp.exp2(scores * log_scale - top)
            summed = probs.sum(axis=-1, keepdims=True)
            product = dot_nn(probs.astype(BF16), kv_ref[0, 1, cols, :])
            weight = summed if weight is None else weight + summed
            total = product if total is None else total + product
        out_ref[0, 0, rows, :] = total * (1.0 / weight)
        lse_ref[0, 0, rows, :] = jnp.broadcast_to(top + jnp.log2(weight), total.shape)


def own_forward(queries, own_kv, softmax_scale):
    kv_count, groups, rows, width = queries.shape
    by_group = pl.BlockSpec((1, 1, rows, width), lambda n, g: (n, g, 0, 0))
    return pl.pallas_call(
        functools.partial(own_forward_kernel, softmax_scale * math.log2(math.e)),
        grid=(kv_count, groups),
        out_shape=(
            jax.ShapeDtypeStruct(queries.shape, F32),
            jax.ShapeDtypeStruct(queries.shape, F32),
        ),
        in_specs=[by_group, pl.BlockSpec((1, 2, rows, width), lambda n, g: (n, 0, 0, 0))],
        out_specs=(by_group, by_group),
        compiler_params=pltpu.CompilerParams(vmem_limit_bytes=24 * MIB),
        cost_estimate=pl.CostEstimate(
            flops=4 * kv_count * groups * rows * rows * width,
            bytes_accessed=12 * kv_count * groups * rows * width,
            transcendentals=kv_count * groups * rows * rows,
        ),
        name="own_forward",
    )(queries, own_kv)


def near_kernel(
    softmax_scale,
    tiles,
    seen_ref,
    q_ref,
    do_ref,
    near_ref,
    own_out_ref,
    own_lse_ref,
    out_ref,
    stat_ref,
    dq_ref,
    dnear_ref,
    dk_acc,
    dv_acc,
):
    log_scale = softmax_scale * math.log2(math.e)
    groups, _, piece, width = near_ref.shape[2:]
    rows = groups * piece
    step = pl.program_id(1)
    query = q_ref[0]
    grads = do_ref[0]
    keys = [near_ref[0, 0, :, j].reshape(rows, width) for j in range(2)]
    values = [near_ref[0, 1, :, j].reshape(rows, width) for j in range(2)]
    seen = [seen_ref[j] > 0 for j in range(2)]

    @pl.when(step == 0)
    def _():
        dk_acc[...] = jnp.zeros_like(dk_acc)
        dv_acc[...] = jnp.zeros_like(dv_acc)

    own_lse = own_lse_ref[0][:, :1]
    scores = [dot_nt(query, keys[j]) for j in range(2)]
    top = own_lse
    for j in range(2):
        peak = scores[j].max(axis=-1, keepdims=True) * log_scale
        top = jnp.maximum(top, jnp.where(seen[j], peak, -jnp.inf))
    own_share = jnp.exp2(own_lse - top)
    weight = own_share
    total = own_share * own_out_ref[0]
    probs, low = [], []
    for j in range(2):
        shift = jnp.where(seen[j], top, jnp.inf)
        probs.append(jnp.exp2(scores[j] * log_scale - shift))
        weight = weight + probs[j].sum(axis=-1, keepdims=True)
        low.append(probs[j].astype(BF16))
        total = total + dot_nn(low[j], values[j])
    inverse = 1.0 / weight
    head_out = (total * inverse).astype(BF16)
    out_ref[0] = head_out
    grads_f = grads.astype(F32)
    row_dot = jnp.sum(grads_f * head_out.astype(F32), axis=-1, keepdims=True)
    lane = lax.broadcasted_iota(jnp.int32, (query.shape[0], width), 1)
    stat_ref[0] = jnp.where(lane < width // 2, top + jnp.log2(weight), row_dot)
    grads_low = (grads_f * inverse).astype(BF16)
    shift_dot = row_dot * inverse
    dq = None
    for j in range(2):
        grad_probs = dot_nt(grads_low, values[j])
        grad_scores = (probs[j] * (grad_probs - shift_dot)).astype(BF16)
        term = dot_nn(grad_scores, keys[j])
        dq = term if dq is None else dq + term
        dk_acc[j] += dot_tn(grad_scores, query)
        dv_acc[j] += dot_tn(low[j], grads_low)
    dq_ref[0] = dq

    @pl.when(step == tiles - 1)
    def _():
        for j in range(2):
            dnear_ref[0, 0, :, j] = (
                (dk_acc[j] * softmax_scale).astype(BF16).reshape(groups, piece, width)
            )
            dnear_ref[0, 1, :, j] = dv_acc[j].astype(BF16).reshape(groups, piece, width)


def near_attention(seen, queries, grads, near, own_out, own_lse, softmax_scale, tile):
    kv_count, rows, width = queries.shape
    tiles = rows // tile
    _, _, groups, _, piece, _ = near.shape
    by_tile = pl.BlockSpec((1, tile, width), lambda n, i: (n, i, 0))
    by_head = pl.BlockSpec((1,) + near.shape[1:], lambda n, i: (n, 0, 0, 0, 0, 0))
    return pl.pallas_call(
        functools.partial(near_kernel, softmax_scale, tiles),
        grid=(kv_count, tiles),
        out_shape=(
            jax.ShapeDtypeStruct(queries.shape, BF16),
            jax.ShapeDtypeStruct(queries.shape, F32),
            jax.ShapeDtypeStruct(queries.shape, F32),
            jax.ShapeDtypeStruct(near.shape, BF16),
        ),
        in_specs=[
            pl.BlockSpec(memory_space=pltpu.SMEM),
            by_tile,
            by_tile,
            by_head,
            by_tile,
            by_tile,
        ],
        out_specs=(by_tile, by_tile, by_tile, by_head),
        scratch_shapes=[
            pltpu.VMEM((2, groups * piece, width), F32),
            pltpu.VMEM((2, groups * piece, width), F32),
        ],
        compiler_params=pltpu.CompilerParams(vmem_limit_bytes=40 * MIB),
        cost_estimate=pl.CostEstimate(
            flops=20 * kv_count * rows * groups * piece * width,
            bytes_accessed=20 * kv_count * rows * width,
            transcendentals=2 * kv_count * rows * groups * piece,
        ),
        name="near_attention",
    )(seen, queries, grads, near, own_out, own_lse)


def own_backward_kernel(
    softmax_scale, groups, q_ref, do_ref, kv_ref, stat_ref, dq_near_ref, dq_ref, dkv_ref
):
    log_scale = softmax_scale * math.log2(math.e)
    half = q_ref.shape[2] // 2
    width = q_ref.shape[3]
    step = pl.program_id(1)
    triangle = lower_triangle(half)

    @pl.when(step == 0)
    def _():
        dkv_ref[...] = jnp.zeros_like(dkv_ref)

    for tile in range(2):
        rows = slice(tile * half, (tile + 1) * half)
        query = q_ref[0, 0, rows, :]
        grads = do_ref[0, 0, rows, :]
        lse = stat_ref[0, 0, rows, :1]
        row_dot = stat_ref[0, 0, rows, width // 2 : width // 2 + 1]
        dq = dq_near_ref[0, 0, rows, :]
        for col in range(tile + 1):
            cols = slice(col * half, (col + 1) * half)
            keys = kv_ref[0, 0, cols, :]
            probs = jnp.exp2(dot_nt(query, keys) * log_scale - lse)
            if col == tile:
                probs = jnp.where(triangle, probs, 0.0)
            grad_probs = dot_nt(grads, kv_ref[0, 1, cols, :])
            grad_scores = (probs * (grad_probs - row_dot)).astype(BF16)
            dq = dq + dot_nn(grad_scores, keys)
            dkv_ref[0, 0, cols, :] += dot_tn(grad_scores, query)
            dkv_ref[0, 1, cols, :] += dot_tn(probs.astype(BF16), grads)
        dq_ref[0, 0, rows, :] = (dq * softmax_scale).astype(BF16)

    @pl.when(step == groups - 1)
    def _():
        dkv_ref[0, 0] = dkv_ref[0, 0] * softmax_scale


def own_backward(queries, grads, own_kv, stat, dq_near, softmax_scale):
    kv_count, groups, rows, width = queries.shape
    by_group = pl.BlockSpec((1, 1, rows, width), lambda n, g: (n, g, 0, 0))
    by_head = pl.BlockSpec((1, 2, rows, width), lambda n, g: (n, 0, 0, 0))
    return pl.pallas_call(
        functools.partial(own_backward_kernel, softmax_scale, groups),
        grid=(kv_count, groups),
        out_shape=(
            jax.ShapeDtypeStruct(queries.shape, BF16),
            jax.ShapeDtypeStruct(own_kv.shape, F32),
        ),
        in_specs=[by_group, by_group, by_head, by_group, by_group],
        out_specs=(by_group, by_head),
        compiler_params=pltpu.CompilerParams(vmem_limit_bytes=24 * MIB),
        cost_estimate=pl.CostEstimate(
            flops=10 * kv_count * groups * rows * rows * width,
            bytes_accessed=16 * kv_count * groups * rows * width,
            transcendentals=kv_count * groups * rows * rows,
        ),
        name="own_backward",
    )(queries, grads, own_kv, stat, dq_near)


def exchange(pieces):
    return lax.ppermute(pieces, "head", [(0, 1), (1, 0)])


def spread(pieces):
    return lax.all_to_all(pieces, "ctx", split_axis=0, concat_axis=0, tiled=True)


def on_device(queries, keys, values, output_gradient, selected):
    rows_block, own_groups, kv_count, width = queries.shape
    blocks = lax.axis_size("ctx")
    own_index = lax.axis_index("ctx")
    core = lax.axis_index("head")
    half_kv = kv_count // 2
    mine, theirs = core * half_kv, (1 - core) * half_kv
    softmax_scale = width ** (-0.5)
    piece_groups = blocks // (2 * half_kv)
    piece = rows_block // piece_groups
    picks = selected.reshape(-1)
    own_picks = lax.dynamic_index_in_dim(selected, own_index, 0, keepdims=False)
    seen = (own_picks < own_index).astype(jnp.int32)

    both = jnp.stack([keys, values], axis=0)
    both = lax.dynamic_slice_in_dim(both, mine, half_kv, axis=2)
    own_kv = jnp.transpose(both, (2, 0, 1, 3))
    held = spread(own_kv.reshape(blocks, piece, width))

    inputs = jnp.transpose(jnp.stack([queries, output_gradient], axis=0), (0, 3, 2, 1, 4))
    kept = lax.dynamic_slice_in_dim(inputs, mine, half_kv, axis=1)
    fetched = exchange(lax.dynamic_slice_in_dim(inputs, theirs, half_kv, axis=1))
    inputs = jnp.concatenate([kept, fetched], axis=2)
    q_all, do_all = inputs[0], inputs[1]
    own_out, own_lse = own_forward(q_all, own_kv, softmax_scale)

    near = spread(pick_pieces(held, picks))
    near = near.reshape(half_kv, 2, piece_groups, 2, piece, width)
    flat = (half_kv, 2 * own_groups * rows_block, width)
    attn, stat, dq_near, dnear = near_attention(
        seen,
        q_all.reshape(flat),
        do_all.reshape(flat),
        near,
        own_out.reshape(flat),
        own_lse.reshape(flat),
        softmax_scale,
        rows_block,
    )
    arrived = spread(dnear.reshape(blocks, 2 * piece, width))
    dq, dkv = own_backward(
        q_all, do_all, own_kv, stat.reshape(q_all.shape), dq_near.reshape(q_all.shape), softmax_scale
    )
    home = spread(collect_pieces(arrived, picks))

    def give_back(result):
        result = result.reshape(half_kv, 2 * own_groups, rows_block, width)
        back = exchange(result[:, own_groups:])
        whole = jnp.zeros((kv_count,) + back.shape[1:], result.dtype)
        whole = lax.dynamic_update_slice_in_dim(whole, result[:, :own_groups], mine, 0)
        whole = lax.dynamic_update_slice_in_dim(whole, back, theirs, 0)
        return jnp.transpose(whole, (2, 1, 0, 3))

    attn_out = give_back(attn)
    grad_q = give_back(dq)
    grads = (home.reshape(own_kv.shape).astype(F32) + dkv).astype(BF16)
    grad_k, grad_v = (jnp.transpose(grads[:, part], (1, 0, 2)) for part in range(2))
    return (attn_out, grad_q, grad_k, grad_v)


def solution(mesh):
    return jax.shard_map(
        on_device,
        mesh=mesh,
        in_specs=(
            P("ctx", "head", None, None),
            P("ctx", None, None),
            P("ctx", None, None),
            P("ctx", "head", None, None),
            P(),
        ),
        out_specs=(
            P("ctx", "head", None, None),
            P("ctx", "head", None, None),
            P("ctx", "head", None),
            P("ctx", "head", None),
        ),
        check_vma=False,
    )
```

```python
import functools
import math

import jax
import jax.numpy as jnp
from jax import lax
from jax.experimental import pallas as pl
from jax.experimental.pallas import tpu as pltpu
from jax.sharding import PartitionSpec as P

F32 = jnp.float32
BF16 = jnp.bfloat16
GRANT = 60 * 1024 * 1024
SMALL_GRANT = 8 * 1024 * 1024


def dot_nn(a, b):
    return lax.dot_general(a, b, (((1,), (0,)), ((), ())), preferred_element_type=F32)


def dot_nt(a, b):
    return lax.dot_general(a, b, (((1,), (1,)), ((), ())), preferred_element_type=F32)


def dot_tn(a, b):
    return lax.dot_general(a, b, (((0,), (0,)), ((), ())), preferred_element_type=F32)


def pick_kernel(picks, held, out):
    count, rows2, _ = out.shape
    rows = rows2 // 2
    first = pl.program_id(0) * count

    def body(step, _):
        for sub in range(8):
            at = step * 8 + sub
            for j in range(2):
                out[at, j * rows : (j + 1) * rows, :] = held[picks[(first + at) * 2 + j]]
        return 0

    lax.fori_loop(0, count // 8, body, 0)


def pick_pieces(held, picks):
    blocks, rows, width = held.shape
    steps = 2 if blocks % 16 == 0 else 1
    return pl.pallas_call(
        pick_kernel,
        grid=(steps,),
        out_shape=jax.ShapeDtypeStruct((blocks, 2 * rows, width), held.dtype),
        in_specs=[
            pl.BlockSpec(memory_space=pltpu.SMEM),
            pl.BlockSpec((blocks, rows, width), lambda i: (0, 0, 0)),
        ],
        out_specs=pl.BlockSpec((blocks // steps, 2 * rows, width), lambda i: (i, 0, 0)),
        compiler_params=pltpu.CompilerParams(vmem_limit_bytes=SMALL_GRANT),
        name="pick_pieces",
    )(picks, held)


def collect_kernel(picks, arrived, out, total):
    count, rows2, _ = arrived.shape
    rows = rows2 // 2
    part = pl.program_id(0)

    @pl.when(part == 0)
    def _():
        total[...] = jnp.zeros_like(total)

    def body(step, _):
        for sub in range(8):
            at = step * 8 + sub
            for j in range(2):
                owner = picks[(part * count + at) * 2 + j]
                total[j, owner] += arrived[at, j * rows : (j + 1) * rows, :].astype(F32)
        return 0

    lax.fori_loop(0, count // 8, body, 0)

    @pl.when(part == pl.num_programs(0) - 1)
    def _():
        out[...] = (total[0] + total[1]).astype(out.dtype)


def collect_pieces(arrived, picks):
    blocks, rows2, width = arrived.shape
    steps = 2 if blocks % 16 == 0 else 1
    return pl.pallas_call(
        collect_kernel,
        grid=(steps,),
        out_shape=jax.ShapeDtypeStruct((blocks, rows2 // 2, width), arrived.dtype),
        in_specs=[
            pl.BlockSpec(memory_space=pltpu.SMEM),
            pl.BlockSpec((blocks // steps, rows2, width), lambda i: (i, 0, 0)),
        ],
        out_specs=pl.BlockSpec((blocks, rows2 // 2, width), lambda i: (0, 0, 0)),
        scratch_shapes=[pltpu.VMEM((2, blocks, rows2 // 2, width), F32)],
        compiler_params=pltpu.CompilerParams(vmem_limit_bytes=SMALL_GRANT),
        name="collect_pieces",
    )(picks, arrived)


def causal_pairs(rows):
    return lax.broadcasted_iota(jnp.int32, (rows, rows), 0) <= lax.broadcasted_iota(
        jnp.int32, (rows, rows), 1
    )


def own_forward_kernel(log_scale, q_ref, do_ref, kv_ref, qt_ref, dot_ref, out_ref, lse_ref, vt):
    width = kv_ref.shape[3]
    half = kv_ref.shape[2] // 2
    seen = causal_pairs(half)

    @pl.when(pl.program_id(1) == 0)
    def _():
        vt[...] = kv_ref[0, 1].T

    qt_ref[0] = q_ref[0, 0].T
    dot_ref[0] = do_ref[0, 0].T
    for tile in range(2):
        span = slice(tile * half, (tile + 1) * half)
        query = qt_ref[0, :, span]
        parts = []
        for col in range(tile + 1):
            scores = dot_nn(kv_ref[0, 0, col * half : (col + 1) * half, :], query)
            if col == tile:
                scores = jnp.where(seen, scores, -jnp.inf)
            parts.append(scores)
        top = parts[0].max(axis=0, keepdims=True)
        for scores in parts[1:]:
            top = jnp.maximum(top, scores.max(axis=0, keepdims=True))
        top = top * log_scale
        weight = jnp.zeros_like(top)
        total = jnp.zeros((width, half), F32)
        for col, scores in enumerate(parts):
            probs = jnp.exp2(scores * log_scale - top)
            weight = weight + probs.sum(axis=0, keepdims=True)
            total = total + dot_nn(vt[:, col * half : (col + 1) * half], probs.astype(BF16))
        out_ref[0, :, span] = total * (1.0 / weight)
        lse_ref[0, :, span] = jnp.broadcast_to(top + jnp.log2(weight), (8, half))


def own_forward(queries, grads, own_kv, softmax_scale):
    kv_count, groups, rows, width = queries.shape
    by_group = pl.BlockSpec((1, 1, rows, width), lambda n, g: (n, g, 0, 0))
    turned = pl.BlockSpec((1, width, rows), lambda n, g: (n, 0, g))
    return pl.pallas_call(
        functools.partial(own_forward_kernel, softmax_scale * math.log2(math.e)),
        grid=(kv_count, groups),
        out_shape=(
            jax.ShapeDtypeStruct((kv_count, width, groups * rows), BF16),
            jax.ShapeDtypeStruct((kv_count, width, groups * rows), BF16),
            jax.ShapeDtypeStruct((kv_count, width, groups * rows), F32),
            jax.ShapeDtypeStruct((kv_count, 8, groups * rows), F32),
        ),
        in_specs=[
            by_group,
            by_group,
            pl.BlockSpec((1, 2, rows, width), lambda n, g: (n, 0, 0, 0)),
        ],
        out_specs=(turned, turned, turned, pl.BlockSpec((1, 8, rows), lambda n, g: (n, 0, g))),
        scratch_shapes=[pltpu.VMEM((width, rows), BF16)],
        compiler_params=pltpu.CompilerParams(vmem_limit_bytes=GRANT),
        cost_estimate=pl.CostEstimate(
            flops=4 * kv_count * groups * rows * rows * width,
            bytes_accessed=12 * kv_count * groups * rows * width,
            transcendentals=kv_count * groups * rows * rows,
        ),
        name="own_forward",
    )(queries, grads, own_kv)


def near_kernel(
    softmax_scale,
    tiles,
    seen_ref,
    q_ref,
    qt_ref,
    dot_ref,
    near_ref,
    own_out_ref,
    own_lse_ref,
    out_ref,
    lse_ref,
    row_dot_ref,
    dq_ref,
    dnear_ref,
    dk_acc,
    dv_acc,
    kt,
    vt,
):
    log_scale = softmax_scale * math.log2(math.e)
    groups, _, piece, width = near_ref.shape[2:]
    rows = groups * piece
    step = pl.program_id(1)
    keys = [near_ref[0, 0, :, j].reshape(rows, width) for j in range(2)]
    values = [near_ref[0, 1, :, j].reshape(rows, width) for j in range(2)]
    seen = [seen_ref[j] > 0 for j in range(2)]

    @pl.when(step == 0)
    def _():
        dk_acc[...] = jnp.zeros_like(dk_acc)
        dv_acc[...] = jnp.zeros_like(dv_acc)
        for j in range(2):
            kt[j] = keys[j].T
            vt[j] = values[j].T

    query = qt_ref[0]
    own_lse = own_lse_ref[0, :1]
    scores = [dot_nn(keys[j], query) for j in range(2)]
    top = own_lse
    for j in range(2):
        peak = scores[j].max(axis=0, keepdims=True) * log_scale
        top = jnp.maximum(top, jnp.where(seen[j], peak, -jnp.inf))
    own_share = jnp.exp2(own_lse - top)
    weight = own_share
    total = own_share * own_out_ref[0]
    probs, low = [], []
    for j in range(2):
        shift = jnp.where(seen[j], top, jnp.inf)
        probs.append(jnp.exp2(scores[j] * log_scale - shift))
        weight = weight + probs[j].sum(axis=0, keepdims=True)
        low.append(probs[j].astype(BF16))
        total = total + dot_nn(vt[j], low[j])
    inverse = 1.0 / weight
    head_out = (total * inverse).astype(BF16)
    out_ref[0] = head_out
    grads_f = dot_ref[0].astype(F32)
    row_dot = jnp.sum(grads_f * head_out.astype(F32), axis=0, keepdims=True)
    lse_ref[0] = jnp.broadcast_to(top + jnp.log2(weight), lse_ref.shape[1:])
    row_dot_ref[0] = jnp.broadcast_to(row_dot, row_dot_ref.shape[1:])
    grads_low = (grads_f * inverse).astype(BF16)
    grads_rows = grads_low.T
    shift_dot = row_dot * inverse
    dq = None
    for j in range(2):
        grad_probs = dot_nn(values[j], grads_low)
        grad_scores = (probs[j] * (grad_probs - shift_dot)).astype(BF16)
        dv_acc[j] += dot_nn(low[j], grads_rows)
        dk_acc[j] += dot_nn(grad_scores, q_ref[0])
        term = dot_nn(kt[j], grad_scores)
        dq = term if dq is None else dq + term
    dq_ref[0] = dq

    @pl.when(step == tiles - 1)
    def _():
        for j in range(2):
            dnear_ref[0, 0, :, j] = (
                (dk_acc[j] * softmax_scale).astype(BF16).reshape(groups, piece, width)
            )
            dnear_ref[0, 1, :, j] = dv_acc[j].astype(BF16).reshape(groups, piece, width)


def near_attention(seen, queries, turned_q, turned_do, near, own_out, own_lse, softmax_scale, tile):
    kv_count, rows, width = queries.shape
    tiles = rows // tile
    _, _, groups, _, piece, _ = near.shape
    key_rows = groups * piece
    by_row = pl.BlockSpec((1, tile, width), lambda n, i: (n, i, 0))
    turned = pl.BlockSpec((1, width, tile), lambda n, i: (n, 0, i))
    stat = pl.BlockSpec((1, 8, tile), lambda n, i: (n, 0, i))
    by_head = pl.BlockSpec((1,) + near.shape[1:], lambda n, i: (n, 0, 0, 0, 0, 0))
    return pl.pallas_call(
        functools.partial(near_kernel, softmax_scale, tiles),
        grid=(kv_count, tiles),
        out_shape=(
            jax.ShapeDtypeStruct((kv_count, width, rows), BF16),
            jax.ShapeDtypeStruct((kv_count, 8, rows), F32),
            jax.ShapeDtypeStruct((kv_count, 8, rows), F32),
            jax.ShapeDtypeStruct((kv_count, width, rows), F32),
            jax.ShapeDtypeStruct(near.shape, BF16),
        ),
        in_specs=[
            pl.BlockSpec(memory_space=pltpu.SMEM),
            by_row,
            turned,
            turned,
            by_head,
            turned,
            stat,
        ],
        out_specs=(turned, stat, stat, turned, by_head),
        scratch_shapes=[
            pltpu.VMEM((2, key_rows, width), F32),
            pltpu.VMEM((2, key_rows, width), F32),
            pltpu.VMEM((2, width, key_rows), BF16),
            pltpu.VMEM((2, width, key_rows), BF16),
        ],
        compiler_params=pltpu.CompilerParams(vmem_limit_bytes=GRANT),
        cost_estimate=pl.CostEstimate(
            flops=20 * kv_count * rows * key_rows * width,
            bytes_accessed=20 * kv_count * rows * width,
            transcendentals=2 * kv_count * rows * key_rows,
        ),
        name="near_attention",
    )(seen, queries, turned_q, turned_do, near, own_out, own_lse)


def own_backward_kernel(
    softmax_scale,
    groups,
    q_ref,
    do_ref,
    qt_ref,
    dot_ref,
    kv_ref,
    lse_ref,
    row_dot_ref,
    out_t_ref,
    dq_near_ref,
    rows_ref,
    dkv_ref,
    kt,
):
    log_scale = softmax_scale * math.log2(math.e)
    half = kv_ref.shape[2] // 2
    step = pl.program_id(1)
    seen = causal_pairs(half)

    @pl.when(step == 0)
    def _():
        dkv_ref[...] = jnp.zeros_like(dkv_ref)
        kt[...] = kv_ref[0, 0].T

    rows_ref[0, 0, 0] = out_t_ref[0].T
    for tile in range(2):
        span = slice(tile * half, (tile + 1) * half)
        query = qt_ref[0, :, span]
        grads = dot_ref[0, :, span]
        lse = lse_ref[0, :1, span]
        row_dot = row_dot_ref[0, :1, span]
        dq = dq_near_ref[0, :, span]
        for col in range(tile + 1):
            cols = slice(col * half, (col + 1) * half)
            probs = jnp.exp2(dot_nn(kv_ref[0, 0, cols, :], query) * log_scale - lse)
            if col == tile:
                probs = jnp.where(seen, probs, 0.0)
            grad_probs = dot_nn(kv_ref[0, 1, cols, :], grads)
            grad_scores = (probs * (grad_probs - row_dot)).astype(BF16)
            dq = dq + dot_nn(kt[:, cols], grad_scores)
            dkv_ref[0, 0, cols, :] += dot_nn(grad_scores, q_ref[0, 0, span, :])
            dkv_ref[0, 1, cols, :] += dot_nn(probs.astype(BF16), do_ref[0, 0, span, :])
        rows_ref[1, 0, 0, span, :] = (dq * softmax_scale).astype(BF16).T

    @pl.when(step == groups - 1)
    def _():
        dkv_ref[0, 0] = dkv_ref[0, 0] * softmax_scale


def own_backward(
    queries, grads, turned_q, turned_do, own_kv, lse, row_dot, turned_out, dq_near, softmax_scale
):
    kv_count, groups, rows, width = queries.shape
    by_group = pl.BlockSpec((1, 1, rows, width), lambda n, g: (n, g, 0, 0))
    by_head = pl.BlockSpec((1, 2, rows, width), lambda n, g: (n, 0, 0, 0))
    turned = pl.BlockSpec((1, width, rows), lambda n, g: (n, 0, g))
    stat = pl.BlockSpec((1, 8, rows), lambda n, g: (n, 0, g))
    return pl.pallas_call(
        functools.partial(own_backward_kernel, softmax_scale, groups),
        grid=(kv_count, groups),
        out_shape=(
            jax.ShapeDtypeStruct((2,) + queries.shape, BF16),
            jax.ShapeDtypeStruct(own_kv.shape, F32),
        ),
        in_specs=[by_group, by_group, turned, turned, by_head, stat, stat, turned, turned],
        out_specs=(pl.BlockSpec((2, 1, 1, rows, width), lambda n, g: (0, n, g, 0, 0)), by_head),
        scratch_shapes=[pltpu.VMEM((width, rows), BF16)],
        compiler_params=pltpu.CompilerParams(vmem_limit_bytes=GRANT),
        cost_estimate=pl.CostEstimate(
            flops=10 * kv_count * groups * rows * rows * width,
            bytes_accessed=16 * kv_count * groups * rows * width,
            transcendentals=kv_count * groups * rows * rows,
        ),
        name="own_backward",
    )(queries, grads, turned_q, turned_do, own_kv, lse, row_dot, turned_out, dq_near)


def exchange(pieces):
    return lax.ppermute(pieces, "head", [(0, 1), (1, 0)])


def spread(pieces):
    return lax.all_to_all(pieces, "ctx", split_axis=0, concat_axis=0, tiled=True)


def on_device(queries, keys, values, output_gradient, selected):
    rows_block, own_groups, kv_count, width = queries.shape
    blocks = lax.axis_size("ctx")
    own_index = lax.axis_index("ctx")
    core = lax.axis_index("head")
    half_kv = kv_count // 2
    mine, theirs = core * half_kv, (1 - core) * half_kv
    softmax_scale = width ** (-0.5)
    piece_groups = blocks // (2 * half_kv)
    piece = rows_block // piece_groups
    picks = selected.reshape(-1)
    own_picks = lax.dynamic_index_in_dim(selected, own_index, 0, keepdims=False)
    seen = (own_picks < own_index).astype(jnp.int32)

    both = jnp.stack([keys, values], axis=0)
    both = lax.dynamic_slice_in_dim(both, mine, half_kv, axis=2)
    own_kv = jnp.transpose(both, (2, 0, 1, 3))
    held = spread(own_kv.reshape(blocks, piece, width))

    inputs = jnp.transpose(jnp.stack([queries, output_gradient], axis=0), (0, 3, 2, 1, 4))
    kept = lax.dynamic_slice_in_dim(inputs, mine, half_kv, axis=1)
    fetched = exchange(lax.dynamic_slice_in_dim(inputs, theirs, half_kv, axis=1))
    inputs = jnp.concatenate([kept, fetched], axis=2)
    q_all, do_all = inputs[0], inputs[1]
    turned_q, turned_do, own_out, own_lse = own_forward(q_all, do_all, own_kv, softmax_scale)

    near = spread(pick_pieces(held, picks))
    near = near.reshape(half_kv, 2, piece_groups, 2, piece, width)
    group_rows = 2 * own_groups * rows_block
    turned_out, lse, row_dot, dq_near, dnear = near_attention(
        seen,
        q_all.reshape(half_kv, group_rows, width),
        turned_q,
        turned_do,
        near,
        own_out,
        own_lse,
        softmax_scale,
        group_rows // 2,
    )
    arrived = spread(dnear.reshape(blocks, 2 * piece, width))
    results, dkv = own_backward(
        q_all,
        do_all,
        turned_q,
        turned_do,
        own_kv,
        lse,
        row_dot,
        turned_out,
        dq_near,
        softmax_scale,
    )
    home = spread(collect_pieces(arrived, picks))

    back = exchange(results[:, :, own_groups:])
    whole = jnp.zeros((2, kv_count) + back.shape[2:], results.dtype)
    whole = lax.dynamic_update_slice_in_dim(whole, results[:, :, :own_groups], mine, 1)
    whole = lax.dynamic_update_slice_in_dim(whole, back, theirs, 1)
    attn_out, grad_q = (jnp.transpose(whole[part], (2, 1, 0, 3)) for part in range(2))
    grads = (home.reshape(own_kv.shape).astype(F32) + dkv).astype(BF16)
    grad_k, grad_v = (jnp.transpose(grads[:, part], (1, 0, 2)) for part in range(2))
    return (attn_out, grad_q, grad_k, grad_v)


def solution(mesh):
    return jax.shard_map(
        on_device,
        mesh=mesh,
        in_specs=(
            P("ctx", "head", None, None),
            P("ctx", None, None),
            P("ctx", None, None),
            P("ctx", "head", None, None),
            P(),
        ),
        out_specs=(
            P("ctx", "head", None, None),
            P("ctx", "head", None, None),
            P("ctx", "head", None),
            P("ctx", "head", None),
        ),
        check_vma=False,
    )
```

```python
import functools
import math

import jax
import jax.numpy as jnp
from jax import lax
from jax.experimental import pallas as pl
from jax.experimental.pallas import tpu as pltpu
from jax.sharding import PartitionSpec as P

F32 = jnp.float32
BF16 = jnp.bfloat16
GRANT = 60 * 1024 * 1024
SMALL_GRANT = 8 * 1024 * 1024


def dot_nn(a, b):
    return lax.dot_general(a, b, (((1,), (0,)), ((), ())), preferred_element_type=F32)


def dot_nt(a, b):
    return lax.dot_general(a, b, (((1,), (1,)), ((), ())), preferred_element_type=F32)


def dot_tn(a, b):
    return lax.dot_general(a, b, (((0,), (0,)), ((), ())), preferred_element_type=F32)


def pick_kernel(picks, held, out):
    count, rows2, _ = out.shape
    rows = rows2 // 2
    first = pl.program_id(0) * count

    def body(step, _):
        for sub in range(8):
            at = step * 8 + sub
            for j in range(2):
                out[at, j * rows : (j + 1) * rows, :] = held[picks[(first + at) * 2 + j]]
        return 0

    lax.fori_loop(0, count // 8, body, 0)


def pick_pieces(held, picks):
    blocks, rows, width = held.shape
    steps = 2 if blocks % 16 == 0 else 1
    return pl.pallas_call(
        pick_kernel,
        grid=(steps,),
        out_shape=jax.ShapeDtypeStruct((blocks, 2 * rows, width), held.dtype),
        in_specs=[
            pl.BlockSpec(memory_space=pltpu.SMEM),
            pl.BlockSpec((blocks, rows, width), lambda i: (0, 0, 0)),
        ],
        out_specs=pl.BlockSpec((blocks // steps, 2 * rows, width), lambda i: (i, 0, 0)),
        compiler_params=pltpu.CompilerParams(vmem_limit_bytes=SMALL_GRANT),
        name="pick_pieces",
    )(picks, held)


def collect_kernel(picks, arrived, out, *totals):
    count, rows2, _ = arrived.shape
    rows = rows2 // 2
    part = pl.program_id(0)

    @pl.when(part == 0)
    def _():
        for total in totals:
            total[...] = jnp.zeros_like(total)

    def body(step, _):
        for sub in range(8):
            at = step * 8 + sub
            for j in range(2):
                owner = picks[(part * count + at) * 2 + j]
                totals[j][owner] += arrived[at, j * rows : (j + 1) * rows, :].astype(F32)
        return 0

    lax.fori_loop(0, count // 8, body, 0)

    @pl.when(part == pl.num_programs(0) - 1)
    def _():
        out[...] = (totals[0][...] + totals[1][...]).astype(out.dtype)


def collect_pieces(arrived, picks):
    blocks, rows2, width = arrived.shape
    steps = 2 if blocks % 16 == 0 else 1
    return pl.pallas_call(
        collect_kernel,
        grid=(steps,),
        out_shape=jax.ShapeDtypeStruct((blocks, rows2 // 2, width), arrived.dtype),
        in_specs=[
            pl.BlockSpec(memory_space=pltpu.SMEM),
            pl.BlockSpec((blocks // steps, rows2, width), lambda i: (i, 0, 0)),
        ],
        out_specs=pl.BlockSpec((blocks, rows2 // 2, width), lambda i: (0, 0, 0)),
        scratch_shapes=[pltpu.VMEM((blocks, rows2 // 2, width), F32)] * 2,
        compiler_params=pltpu.CompilerParams(vmem_limit_bytes=SMALL_GRANT),
        name="collect_pieces",
    )(picks, arrived)


def causal_pairs(rows):
    return lax.broadcasted_iota(jnp.int32, (rows, rows), 0) <= lax.broadcasted_iota(
        jnp.int32, (rows, rows), 1
    )


def own_forward_kernel(log_scale, q_ref, do_ref, kv_ref, qt_ref, dot_ref, lse_ref, row_dot_ref, vt):
    width = kv_ref.shape[3]
    half = kv_ref.shape[2] // 2
    seen = causal_pairs(half)

    @pl.when(pl.program_id(1) == 0)
    def _():
        vt[...] = kv_ref[0, 1].T

    turned_do = do_ref[0, 0].T
    qt_ref[0] = q_ref[0, 0].T
    dot_ref[0] = turned_do
    for tile in range(2):
        span = slice(tile * half, (tile + 1) * half)
        query = qt_ref[0, :, span]
        parts = []
        for col in range(tile + 1):
            scores = dot_nn(kv_ref[0, 0, col * half : (col + 1) * half, :], query)
            if col == tile:
                scores = jnp.where(seen, scores, -jnp.inf)
            parts.append(scores)
        top = parts[0].max(axis=0, keepdims=True)
        for scores in parts[1:]:
            top = jnp.maximum(top, scores.max(axis=0, keepdims=True))
        top = top * log_scale
        weight = jnp.zeros_like(top)
        total = jnp.zeros((width, half), F32)
        for col, scores in enumerate(parts):
            probs = jnp.exp2(scores * log_scale - top)
            weight = weight + probs.sum(axis=0, keepdims=True)
            total = total + dot_nn(vt[:, col * half : (col + 1) * half], probs.astype(BF16))
        row_dot = jnp.sum(total * turned_do[:, span].astype(F32), axis=0, keepdims=True) / weight
        lse_ref[0, :, span] = jnp.broadcast_to(top + jnp.log2(weight), (8, half))
        row_dot_ref[0, :, span] = jnp.broadcast_to(row_dot, (8, half))


def own_forward(queries, grads, own_kv, softmax_scale):
    kv_count, groups, rows, width = queries.shape
    by_group = pl.BlockSpec((1, 1, rows, width), lambda n, g: (n, g, 0, 0))
    turned = pl.BlockSpec((1, width, rows), lambda n, g: (n, 0, g))
    stat = pl.BlockSpec((1, 8, rows), lambda n, g: (n, 0, g))
    return pl.pallas_call(
        functools.partial(own_forward_kernel, softmax_scale * math.log2(math.e)),
        grid=(kv_count, groups),
        out_shape=(
            jax.ShapeDtypeStruct((kv_count, width, groups * rows), BF16),
            jax.ShapeDtypeStruct((kv_count, width, groups * rows), BF16),
            jax.ShapeDtypeStruct((kv_count, 8, groups * rows), F32),
            jax.ShapeDtypeStruct((kv_count, 8, groups * rows), F32),
        ),
        in_specs=[
            by_group,
            by_group,
            pl.BlockSpec((1, 2, rows, width), lambda n, g: (n, 0, 0, 0)),
        ],
        out_specs=(turned, turned, stat, stat),
        scratch_shapes=[pltpu.VMEM((width, rows), BF16)],
        compiler_params=pltpu.CompilerParams(vmem_limit_bytes=GRANT),
        cost_estimate=pl.CostEstimate(
            flops=4 * kv_count * groups * rows * rows * width,
            bytes_accessed=12 * kv_count * groups * rows * width,
            transcendentals=kv_count * groups * rows * rows,
        ),
        name="own_forward",
    )(queries, grads, own_kv)


def near_kernel(
    softmax_scale,
    tile,
    seen_ref,
    qt_ref,
    dot_ref,
    near_ref,
    own_lse_ref,
    own_dot_ref,
    lse_ref,
    row_dot_ref,
    dnear_ref,
    dk_acc,
    dv_acc,
):
    log_scale = softmax_scale * math.log2(math.e)
    groups, _, piece, width = near_ref.shape[2:]
    rows = groups * piece
    seen = [seen_ref[j] > 0 for j in range(2)]
    count = qt_ref.shape[2] // tile
    held = [{} for _ in range(count)]
    dk_acc[...] = jnp.zeros_like(dk_acc)
    dv_acc[...] = jnp.zeros_like(dv_acc)

    def span(at):
        return slice(at * tile, (at + 1) * tile)

    def score(at, j):
        scores = dot_nn(near_ref[0, 0, :, j].reshape(rows, width), qt_ref[0, :, span(at)])
        held[at]["scores", j] = scores
        held[at]["peak", j] = scores.max(axis=0, keepdims=True) * log_scale

    def settle(at):
        own_lse = own_lse_ref[0, :1, span(at)]
        top = own_lse
        for j in range(2):
            top = jnp.maximum(top, jnp.where(seen[j], held[at].pop(("peak", j)), -jnp.inf))
        share = jnp.exp2(own_lse - top)
        held[at]["top"] = top
        held[at]["weight"] = share
        held[at]["dot"] = share * own_dot_ref[0, :1, span(at)]

    def weigh(at, j):
        grad_probs = dot_nn(near_ref[0, 1, :, j].reshape(rows, width), dot_ref[0, :, span(at)])
        shift = jnp.where(seen[j], held[at]["top"], jnp.inf)
        probs = jnp.exp2(held[at].pop(("scores", j)) * log_scale - shift)
        held[at]["weight"] += probs.sum(axis=0, keepdims=True)
        held[at]["dot"] += (probs * grad_probs).sum(axis=0, keepdims=True)
        held[at]["low", j] = probs.astype(BF16)
        held[at]["grad_probs", j] = grad_probs

    def normalise(at):
        weight = held[at]["weight"]
        inverse = 1.0 / weight
        row_dot = held[at]["dot"] * inverse
        held[at]["row_dot"] = row_dot
        lse = held[at]["top"] + jnp.log2(weight)
        lse_ref[0, :, span(at)] = jnp.broadcast_to(lse, (8, tile))
        row_dot_ref[0, :, span(at)] = jnp.broadcast_to(row_dot, (8, tile))
        held[at]["grads"] = (dot_ref[0, :, span(at)].astype(F32) * inverse).astype(BF16).T
        held[at]["query"] = (qt_ref[0, :, span(at)].astype(F32) * inverse).astype(BF16).T

    def differ(at, j):
        change = held[at].pop(("grad_probs", j)) - held[at]["row_dot"]
        held[at]["grad_scores", j] = held[at]["low", j] * change.astype(BF16)

    def gather(at, j):
        dv_acc[j] += dot_nn(held[at].pop(("low", j)), held[at]["grads"])
        dk_acc[j] += dot_nn(held[at].pop(("grad_scores", j)), held[at]["query"])

    def stage(step, at, *parts):
        if 0 <= at < count:
            step(at, *parts)

    for at in range(count + 3):
        stage(settle, at - 1)
        stage(normalise, at - 2)
        for j in range(2):
            stage(gather, at - 3, j)
            stage(score, at, j)
            stage(weigh, at - 1, j)
            stage(differ, at - 2, j)

    for j in range(2):
        dnear_ref[0, 0, :, j] = (
            (dk_acc[j] * softmax_scale).astype(BF16).reshape(groups, piece, width)
        )
        dnear_ref[0, 1, :, j] = dv_acc[j].astype(BF16).reshape(groups, piece, width)


def near_attention(seen, turned_q, turned_do, near, own_lse, own_dot, softmax_scale, tile):
    kv_count, width, rows = turned_q.shape
    _, _, groups, _, piece, _ = near.shape
    key_rows = groups * piece
    turned = pl.BlockSpec((1, width, rows), lambda n: (n, 0, 0))
    stat = pl.BlockSpec((1, 8, rows), lambda n: (n, 0, 0))
    by_head = pl.BlockSpec((1,) + near.shape[1:], lambda n: (n, 0, 0, 0, 0, 0))
    return pl.pallas_call(
        functools.partial(near_kernel, softmax_scale, tile),
        grid=(kv_count,),
        out_shape=(
            jax.ShapeDtypeStruct((kv_count, 8, rows), F32),
            jax.ShapeDtypeStruct((kv_count, 8, rows), F32),
            jax.ShapeDtypeStruct(near.shape, BF16),
        ),
        in_specs=[pl.BlockSpec(memory_space=pltpu.SMEM), turned, turned, by_head, stat, stat],
        out_specs=(stat, stat, by_head),
        scratch_shapes=[
            pltpu.VMEM((2, key_rows, width), F32),
            pltpu.VMEM((2, key_rows, width), F32),
        ],
        compiler_params=pltpu.CompilerParams(vmem_limit_bytes=GRANT),
        cost_estimate=pl.CostEstimate(
            flops=16 * kv_count * rows * key_rows * width,
            bytes_accessed=10 * kv_count * rows * width,
            transcendentals=2 * kv_count * rows * key_rows,
        ),
        name="near_attention",
    )(seen, turned_q, turned_do, near, own_lse, own_dot)


def finish_kernel(
    softmax_scale,
    seen_ref,
    q_ref,
    do_ref,
    qt_ref,
    dot_ref,
    kv_ref,
    near_ref,
    lse_ref,
    row_dot_ref,
    kept_ref,
    moved_ref,
    dkv_ref,
    turned_kv,
):
    log_scale = softmax_scale * math.log2(math.e)
    group_count, block = q_ref.shape[1:3]
    groups, _, piece, width = near_ref.shape[2:]
    tile = block // 2
    triangle = causal_pairs(tile)
    dkv_ref[...] = jnp.zeros_like(dkv_ref)
    for kind in range(2):
        for j in range(2):
            turned_kv[kind, j] = near_ref[0, kind, :, j].reshape(block, width).T
        turned_kv[kind, 2] = kv_ref[0, kind].T
    items = []
    for at in range(group_count * 2):
        own = [(at, 2, col) for col in range(at % 2 + 1)]
        items += [(at, 0, None), (at, 1, None)] + own
    held = [{} for _ in items]
    sums = {}

    def keys_of(kind, j, col):
        if j < 2:
            return near_ref[0, kind, :, j].reshape(block, width)
        return kv_ref[0, kind, col * tile : (col + 1) * tile, :]

    def turned_of(kind, j, col):
        if j < 2:
            return turned_kv[kind, j]
        return turned_kv[kind, 2, :, col * tile : (col + 1) * tile]

    def score(item):
        at, j, col = items[item]
        held[item]["scores"] = dot_nn(keys_of(0, j, col), qt_ref[0, :, at * tile : (at + 1) * tile])

    def weigh(item):
        at, j, col = items[item]
        span = slice(at * tile, (at + 1) * tile)
        grad_probs = dot_nn(keys_of(1, j, col), dot_ref[0, :, span])
        lse = lse_ref[0, :1, span]
        if j < 2:
            lse = jnp.where(seen_ref[j] > 0, lse, jnp.inf)
        probs = jnp.exp2(held[item].pop("scores") * log_scale - lse)
        if j == 2 and col == at % 2:
            probs = jnp.where(triangle, probs, 0.0)
        held[item]["low"] = probs.astype(BF16)
        held[item]["grad_scores"] = (probs * (grad_probs - row_dot_ref[0, :1, span])).astype(BF16)

    def gather(item):
        at, j, col = items[item]
        low, grad_scores = held[item].pop("low"), held[item].pop("grad_scores")
        for kind, factor in ((1, low), (0, grad_scores)):
            term = dot_nn(turned_of(kind, j, col), factor)
            sums[at, kind] = sums[at, kind] + term if (at, kind) in sums else term
        group, rows = at // 2, slice(at % 2 * tile, (at % 2 + 1) * tile)
        if j == 2:
            cols = slice(col * tile, (col + 1) * tile)
            dkv_ref[0, 0, cols, :] += dot_nn(grad_scores, q_ref[0, group, rows, :])
            dkv_ref[0, 1, cols, :] += dot_nn(low, do_ref[0, group, rows, :])
            if col == at % 2:
                out_ref = kept_ref if 2 * group < group_count else moved_ref
                group = group % (group_count // 2)
                out_ref[0, 0, group, rows, :] = sums.pop((at, 1)).astype(BF16).T
                out_ref[1, 0, group, rows, :] = (
                    (sums.pop((at, 0)) * softmax_scale).astype(BF16).T
                )

    for item in range(len(items) + 2):
        for step, late in ((gather, 2), (score, 0), (weigh, 1)):
            if 0 <= item - late < len(items):
                step(item - late)
    dkv_ref[0, 0] = dkv_ref[0, 0] * softmax_scale


def finish(seen, queries, grads, turned_q, turned_do, own_kv, near, lse, row_dot, softmax_scale):
    kv_count, groups, rows, width = queries.shape
    by_head = pl.BlockSpec((1, groups, rows, width), lambda n: (n, 0, 0, 0))
    own = pl.BlockSpec((1, 2, rows, width), lambda n: (n, 0, 0, 0))
    turned = pl.BlockSpec((1, width, groups * rows), lambda n: (n, 0, 0))
    stat = pl.BlockSpec((1, 8, groups * rows), lambda n: (n, 0, 0))
    half_groups = pl.BlockSpec((2, 1, groups // 2, rows, width), lambda n: (0, n, 0, 0, 0))
    near_head = pl.BlockSpec((1,) + near.shape[1:], lambda n: (n, 0, 0, 0, 0, 0))
    return pl.pallas_call(
        functools.partial(finish_kernel, softmax_scale),
        grid=(kv_count,),
        out_shape=(
            jax.ShapeDtypeStruct((2, kv_count, groups // 2, rows, width), BF16),
            jax.ShapeDtypeStruct((2, kv_count, groups // 2, rows, width), BF16),
            jax.ShapeDtypeStruct(own_kv.shape, F32),
        ),
        in_specs=[
            pl.BlockSpec(memory_space=pltpu.SMEM),
            by_head,
            by_head,
            turned,
            turned,
            own,
            near_head,
            stat,
            stat,
        ],
        out_specs=(half_groups, half_groups, own),
        scratch_shapes=[pltpu.VMEM((2, 3, width, rows), BF16)],
        compiler_params=pltpu.CompilerParams(vmem_limit_bytes=GRANT),
        cost_estimate=pl.CostEstimate(
            flops=26 * kv_count * groups * rows * rows * width,
            bytes_accessed=16 * kv_count * groups * rows * width,
            transcendentals=3 * kv_count * groups * rows * rows,
        ),
        name="finish",
    )(seen, queries, grads, turned_q, turned_do, own_kv, near, lse, row_dot)


def exchange(pieces):
    return lax.ppermute(pieces, "head", [(0, 1), (1, 0)])


def spread(pieces):
    return lax.all_to_all(pieces, "ctx", split_axis=0, concat_axis=0, tiled=True)


def on_device(queries, keys, values, output_gradient, selected):
    rows_block, own_groups, kv_count, width = queries.shape
    blocks = lax.axis_size("ctx")
    own_index = lax.axis_index("ctx")
    core = lax.axis_index("head")
    half_kv = kv_count // 2
    mine, theirs = core * half_kv, (1 - core) * half_kv
    softmax_scale = width ** (-0.5)
    piece_groups = blocks // (2 * half_kv)
    piece = rows_block // piece_groups
    picks = selected.reshape(-1)
    own_picks = lax.dynamic_index_in_dim(selected, own_index, 0, keepdims=False)
    seen = (own_picks < own_index).astype(jnp.int32)

    both = jnp.stack([keys, values], axis=0)
    both = lax.dynamic_slice_in_dim(both, mine, half_kv, axis=2)
    own_kv = jnp.transpose(both, (2, 0, 1, 3))
    held = spread(own_kv.reshape(blocks, piece, width))

    inputs = jnp.transpose(jnp.stack([queries, output_gradient], axis=0), (0, 3, 2, 1, 4))
    kept = lax.dynamic_slice_in_dim(inputs, mine, half_kv, axis=1)
    fetched = exchange(lax.dynamic_slice_in_dim(inputs, theirs, half_kv, axis=1))
    inputs = jnp.concatenate([kept, fetched], axis=2)
    q_all, do_all = inputs[0], inputs[1]
    turned_q, turned_do, own_lse, own_dot = own_forward(q_all, do_all, own_kv, softmax_scale)

    near = spread(pick_pieces(held, picks))
    near = near.reshape(half_kv, 2, piece_groups, 2, piece, width)
    lse, row_dot, dnear = near_attention(
        seen, turned_q, turned_do, near, own_lse, own_dot, softmax_scale, rows_block // 2
    )
    arrived = spread(dnear.reshape(blocks, 2 * piece, width))
    kept, moved, dkv = finish(
        seen, q_all, do_all, turned_q, turned_do, own_kv, near, lse, row_dot, softmax_scale
    )
    home = spread(collect_pieces(arrived, picks))

    back = exchange(moved)
    whole = jnp.zeros((2, kv_count) + back.shape[2:], back.dtype)
    whole = lax.dynamic_update_slice_in_dim(whole, kept, mine, 1)
    whole = lax.dynamic_update_slice_in_dim(whole, back, theirs, 1)
    attn_out, grad_q = (jnp.transpose(whole[part], (2, 1, 0, 3)) for part in range(2))
    grads = (home.reshape(own_kv.shape).astype(F32) + dkv).astype(BF16)
    grad_k, grad_v = (jnp.transpose(grads[:, part], (1, 0, 2)) for part in range(2))
    return (attn_out, grad_q, grad_k, grad_v)


def solution(mesh):
    return jax.shard_map(
        on_device,
        mesh=mesh,
        in_specs=(
            P("ctx", "head", None, None),
            P("ctx", None, None),
            P("ctx", None, None),
            P("ctx", "head", None, None),
            P(),
        ),
        out_specs=(
            P("ctx", "head", None, None),
            P("ctx", "head", None, None),
            P("ctx", "head", None),
            P("ctx", "head", None),
        ),
        check_vma=False,
    )
```

```python
import functools
import math

import jax
import jax.numpy as jnp
from jax import lax
from jax.experimental import pallas as pl
from jax.experimental.pallas import tpu as pltpu
from jax.sharding import PartitionSpec as P

F32 = jnp.float32
BF16 = jnp.bfloat16
GRANT = 60 * 1024 * 1024
SMALL_GRANT = 8 * 1024 * 1024


def dot_nn(a, b):
    return lax.dot_general(a, b, (((1,), (0,)), ((), ())), preferred_element_type=F32)


def dot_nt(a, b):
    return lax.dot_general(a, b, (((1,), (1,)), ((), ())), preferred_element_type=F32)


def dot_tn(a, b):
    return lax.dot_general(a, b, (((0,), (0,)), ((), ())), preferred_element_type=F32)


def pick_kernel(picks, held, out):
    count, rows2, _ = out.shape
    rows = rows2 // 2
    first = pl.program_id(0) * count

    def body(step, _):
        for sub in range(8):
            at = step * 8 + sub
            for j in range(2):
                out[at, j * rows : (j + 1) * rows, :] = held[picks[(first + at) * 2 + j]]
        return 0

    lax.fori_loop(0, count // 8, body, 0)


def pick_pieces(held, picks):
    blocks, rows, width = held.shape
    steps = 2 if blocks % 16 == 0 else 1
    return pl.pallas_call(
        pick_kernel,
        grid=(steps,),
        out_shape=jax.ShapeDtypeStruct((blocks, 2 * rows, width), held.dtype),
        in_specs=[
            pl.BlockSpec(memory_space=pltpu.SMEM),
            pl.BlockSpec((blocks, rows, width), lambda i: (0, 0, 0)),
        ],
        out_specs=pl.BlockSpec((blocks // steps, 2 * rows, width), lambda i: (i, 0, 0)),
        compiler_params=pltpu.CompilerParams(vmem_limit_bytes=SMALL_GRANT),
        name="pick_pieces",
    )(picks, held)


def collect_kernel(picks, arrived, out, *totals):
    count, rows2, _ = arrived.shape
    rows = rows2 // 2
    part = pl.program_id(0)

    @pl.when(part == 0)
    def _():
        for total in totals:
            total[...] = jnp.zeros_like(total)

    def body(step, _):
        for sub in range(8):
            at = step * 8 + sub
            for j in range(2):
                owner = picks[(part * count + at) * 2 + j]
                totals[j][owner] += arrived[at, j * rows : (j + 1) * rows, :].astype(F32)
        return 0

    lax.fori_loop(0, count // 8, body, 0)

    @pl.when(part == pl.num_programs(0) - 1)
    def _():
        out[...] = (totals[0][...] + totals[1][...]).astype(out.dtype)


def collect_pieces(arrived, picks):
    blocks, rows2, width = arrived.shape
    steps = 2 if blocks % 16 == 0 else 1
    return pl.pallas_call(
        collect_kernel,
        grid=(steps,),
        out_shape=jax.ShapeDtypeStruct((blocks, rows2 // 2, width), arrived.dtype),
        in_specs=[
            pl.BlockSpec(memory_space=pltpu.SMEM),
            pl.BlockSpec((blocks // steps, rows2, width), lambda i: (i, 0, 0)),
        ],
        out_specs=pl.BlockSpec((blocks, rows2 // 2, width), lambda i: (0, 0, 0)),
        scratch_shapes=[pltpu.VMEM((blocks, rows2 // 2, width), F32)] * 2,
        compiler_params=pltpu.CompilerParams(vmem_limit_bytes=SMALL_GRANT),
        name="collect_pieces",
    )(picks, arrived)


def causal_pairs(rows):
    return lax.broadcasted_iota(jnp.int32, (rows, rows), 0) <= lax.broadcasted_iota(
        jnp.int32, (rows, rows), 1
    )


def own_forward_kernel(
    log_scale, own_groups, kept_ref, fetched_ref, kv_ref, qt_ref, dot_ref, lse_ref, row_dot_ref, vt
):
    width = kv_ref.shape[3]
    half = kv_ref.shape[2] // 2
    seen = causal_pairs(half)

    @pl.when(pl.program_id(1) == 0)
    def _():
        vt[...] = kv_ref[0, 1].T

    here = pl.program_id(1) < own_groups
    turned_do = jnp.where(here, kept_ref[1, 0, 0], fetched_ref[1, 0, 0]).T
    qt_ref[0] = jnp.where(here, kept_ref[0, 0, 0], fetched_ref[0, 0, 0]).T
    dot_ref[0] = turned_do
    for tile in range(2):
        span = slice(tile * half, (tile + 1) * half)
        query = qt_ref[0, :, span]
        parts = []
        for col in range(tile + 1):
            scores = dot_nn(kv_ref[0, 0, col * half : (col + 1) * half, :], query)
            if col == tile:
                scores = jnp.where(seen, scores, -jnp.inf)
            parts.append(scores)
        top = parts[0].max(axis=0, keepdims=True)
        for scores in parts[1:]:
            top = jnp.maximum(top, scores.max(axis=0, keepdims=True))
        top = top * log_scale
        weight = jnp.zeros_like(top)
        total = jnp.zeros((width, half), F32)
        for col, scores in enumerate(parts):
            probs = jnp.exp2(scores * log_scale - top)
            weight = weight + probs.sum(axis=0, keepdims=True)
            total = total + dot_nn(vt[:, col * half : (col + 1) * half], probs.astype(BF16))
        row_dot = jnp.sum(total * turned_do[:, span].astype(F32), axis=0, keepdims=True) / weight
        lse_ref[0, :, span] = jnp.broadcast_to(top + jnp.log2(weight), (8, half))
        row_dot_ref[0, :, span] = jnp.broadcast_to(row_dot, (8, half))


def own_forward(kept, fetched, own_kv, softmax_scale):
    _, kv_count, own_groups, rows, width = kept.shape
    groups = 2 * own_groups
    one_group = (2, 1, 1, rows, width)
    by_kept = pl.BlockSpec(one_group, lambda n, g: (0, n, jnp.minimum(g, own_groups - 1), 0, 0))
    by_fetched = pl.BlockSpec(one_group, lambda n, g: (0, n, jnp.maximum(g - own_groups, 0), 0, 0))
    turned = pl.BlockSpec((1, width, rows), lambda n, g: (n, 0, g))
    stat = pl.BlockSpec((1, 8, rows), lambda n, g: (n, 0, g))
    return pl.pallas_call(
        functools.partial(own_forward_kernel, softmax_scale * math.log2(math.e), own_groups),
        grid=(kv_count, groups),
        out_shape=(
            jax.ShapeDtypeStruct((kv_count, width, groups * rows), BF16),
            jax.ShapeDtypeStruct((kv_count, width, groups * rows), BF16),
            jax.ShapeDtypeStruct((kv_count, 8, groups * rows), F32),
            jax.ShapeDtypeStruct((kv_count, 8, groups * rows), F32),
        ),
        in_specs=[
            by_kept,
            by_fetched,
            pl.BlockSpec((1, 2, rows, width), lambda n, g: (n, 0, 0, 0)),
        ],
        out_specs=(turned, turned, stat, stat),
        scratch_shapes=[pltpu.VMEM((width, rows), BF16)],
        compiler_params=pltpu.CompilerParams(vmem_limit_bytes=GRANT),
        cost_estimate=pl.CostEstimate(
            flops=4 * kv_count * groups * rows * rows * width,
            bytes_accessed=12 * kv_count * groups * rows * width,
            transcendentals=kv_count * groups * rows * rows,
        ),
        name="own_forward",
    )(kept, fetched, own_kv)


def near_kernel(
    softmax_scale,
    tile,
    seen_ref,
    qt_ref,
    dot_ref,
    near_ref,
    own_lse_ref,
    own_dot_ref,
    lse_ref,
    row_dot_ref,
    dnear_ref,
    dk_acc,
    dv_acc,
):
    log_scale = softmax_scale * math.log2(math.e)
    groups, _, piece, width = near_ref.shape[2:]
    rows = groups * piece
    seen = [seen_ref[j] > 0 for j in range(2)]
    count = qt_ref.shape[2] // tile
    held = [{} for _ in range(count)]
    dk_acc[...] = jnp.zeros_like(dk_acc)
    dv_acc[...] = jnp.zeros_like(dv_acc)

    def span(at):
        return slice(at * tile, (at + 1) * tile)

    def score(at, j):
        scores = dot_nn(near_ref[0, 0, :, j].reshape(rows, width), qt_ref[0, :, span(at)])
        held[at]["scores", j] = scores
        held[at]["peak", j] = scores.max(axis=0, keepdims=True) * log_scale

    def settle(at):
        own_lse = own_lse_ref[0, :1, span(at)]
        top = own_lse
        for j in range(2):
            top = jnp.maximum(top, jnp.where(seen[j], held[at].pop(("peak", j)), -jnp.inf))
        share = jnp.exp2(own_lse - top)
        held[at]["top"] = top
        held[at]["weight"] = share
        held[at]["dot"] = share * own_dot_ref[0, :1, span(at)]

    def weigh(at, j):
        grad_probs = dot_nn(near_ref[0, 1, :, j].reshape(rows, width), dot_ref[0, :, span(at)])
        shift = jnp.where(seen[j], held[at]["top"], jnp.inf)
        probs = jnp.exp2(held[at].pop(("scores", j)) * log_scale - shift)
        held[at]["weight"] += probs.sum(axis=0, keepdims=True)
        held[at]["dot"] += (probs * grad_probs).sum(axis=0, keepdims=True)
        held[at]["low", j] = probs.astype(BF16)
        held[at]["grad_probs", j] = grad_probs

    def normalise(at):
        weight = held[at]["weight"]
        inverse = 1.0 / weight
        row_dot = held[at]["dot"] * inverse
        held[at]["row_dot"] = row_dot
        lse = held[at]["top"] + jnp.log2(weight)
        lse_ref[0, :, span(at)] = jnp.broadcast_to(lse, (8, tile))
        row_dot_ref[0, :, span(at)] = jnp.broadcast_to(row_dot, (8, tile))
        held[at]["grads"] = (dot_ref[0, :, span(at)].astype(F32) * inverse).astype(BF16).T
        held[at]["query"] = (qt_ref[0, :, span(at)].astype(F32) * inverse).astype(BF16).T

    def differ(at, j):
        change = held[at].pop(("grad_probs", j)) - held[at]["row_dot"]
        held[at]["grad_scores", j] = held[at]["low", j] * change.astype(BF16)

    def gather(at, j):
        dv_acc[j] += dot_nn(held[at].pop(("low", j)), held[at]["grads"])
        dk_acc[j] += dot_nn(held[at].pop(("grad_scores", j)), held[at]["query"])

    def stage(step, at, *parts):
        if 0 <= at < count:
            step(at, *parts)

    for at in range(count + 3):
        stage(settle, at - 1)
        stage(normalise, at - 2)
        for j in range(2):
            stage(gather, at - 3, j)
            stage(score, at, j)
            stage(weigh, at - 1, j)
            stage(differ, at - 2, j)

    for j in range(2):
        dnear_ref[0, 0, :, j] = (
            (dk_acc[j] * softmax_scale).astype(BF16).reshape(groups, piece, width)
        )
        dnear_ref[0, 1, :, j] = dv_acc[j].astype(BF16).reshape(groups, piece, width)


def near_attention(seen, turned_q, turned_do, near, own_lse, own_dot, softmax_scale, tile):
    kv_count, width, rows = turned_q.shape
    _, _, groups, _, piece, _ = near.shape
    key_rows = groups * piece
    turned = pl.BlockSpec((1, width, rows), lambda n: (n, 0, 0))
    stat = pl.BlockSpec((1, 8, rows), lambda n: (n, 0, 0))
    by_head = pl.BlockSpec((1,) + near.shape[1:], lambda n: (n, 0, 0, 0, 0, 0))
    return pl.pallas_call(
        functools.partial(near_kernel, softmax_scale, tile),
        grid=(kv_count,),
        out_shape=(
            jax.ShapeDtypeStruct((kv_count, 8, rows), F32),
            jax.ShapeDtypeStruct((kv_count, 8, rows), F32),
            jax.ShapeDtypeStruct(near.shape, BF16),
        ),
        in_specs=[pl.BlockSpec(memory_space=pltpu.SMEM), turned, turned, by_head, stat, stat],
        out_specs=(stat, stat, by_head),
        scratch_shapes=[
            pltpu.VMEM((2, key_rows, width), F32),
            pltpu.VMEM((2, key_rows, width), F32),
        ],
        compiler_params=pltpu.CompilerParams(vmem_limit_bytes=GRANT),
        cost_estimate=pl.CostEstimate(
            flops=16 * kv_count * rows * key_rows * width,
            bytes_accessed=10 * kv_count * rows * width,
            transcendentals=2 * kv_count * rows * key_rows,
        ),
        name="near_attention",
    )(seen, turned_q, turned_do, near, own_lse, own_dot)


def finish_kernel(
    softmax_scale,
    seen_ref,
    mine_ref,
    other_ref,
    qt_ref,
    dot_ref,
    kv_ref,
    near_ref,
    lse_ref,
    row_dot_ref,
    kept_ref,
    moved_ref,
    dkv_ref,
    turned_kv,
):
    log_scale = softmax_scale * math.log2(math.e)
    own_groups, block = mine_ref.shape[2:4]
    group_count = 2 * own_groups
    groups, _, piece, width = near_ref.shape[2:]
    tile = block // 2
    triangle = causal_pairs(tile)
    dkv_ref[...] = jnp.zeros_like(dkv_ref)
    for kind in range(2):
        for j in range(2):
            turned_kv[kind, j] = near_ref[0, kind, :, j].reshape(block, width).T
        turned_kv[kind, 2] = kv_ref[0, kind].T
    items = []
    for at in range(group_count * 2):
        own = [(at, 2, col) for col in range(at % 2 + 1)]
        items += [(at, 0, None), (at, 1, None)] + own
    held = [{} for _ in items]
    sums = {}

    def keys_of(kind, j, col):
        if j < 2:
            return near_ref[0, kind, :, j].reshape(block, width)
        return kv_ref[0, kind, col * tile : (col + 1) * tile, :]

    def turned_of(kind, j, col):
        if j < 2:
            return turned_kv[kind, j]
        return turned_kv[kind, 2, :, col * tile : (col + 1) * tile]

    def score(item):
        at, j, col = items[item]
        held[item]["scores"] = dot_nn(keys_of(0, j, col), qt_ref[0, :, at * tile : (at + 1) * tile])

    def weigh(item):
        at, j, col = items[item]
        span = slice(at * tile, (at + 1) * tile)
        grad_probs = dot_nn(keys_of(1, j, col), dot_ref[0, :, span])
        lse = lse_ref[0, :1, span]
        if j < 2:
            lse = jnp.where(seen_ref[j] > 0, lse, jnp.inf)
        probs = jnp.exp2(held[item].pop("scores") * log_scale - lse)
        if j == 2 and col == at % 2:
            probs = jnp.where(triangle, probs, 0.0)
        held[item]["low"] = probs.astype(BF16)
        held[item]["grad_scores"] = (probs * (grad_probs - row_dot_ref[0, :1, span])).astype(BF16)

    def gather(item):
        at, j, col = items[item]
        low, grad_scores = held[item].pop("low"), held[item].pop("grad_scores")
        for kind, factor in ((1, low), (0, grad_scores)):
            term = dot_nn(turned_of(kind, j, col), factor)
            sums[at, kind] = sums[at, kind] + term if (at, kind) in sums else term
        group, rows = at // 2, slice(at % 2 * tile, (at % 2 + 1) * tile)
        if j == 2:
            rows_ref = mine_ref if group < own_groups else other_ref
            cols = slice(col * tile, (col + 1) * tile)
            dkv_ref[0, 0, cols, :] += dot_nn(grad_scores, rows_ref[0, 0, group % own_groups, rows, :])
            dkv_ref[0, 1, cols, :] += dot_nn(low, rows_ref[1, 0, group % own_groups, rows, :])
            if col == at % 2:
                out_ref = kept_ref if group < own_groups else moved_ref
                group = group % own_groups
                out_ref[0, 0, group, rows, :] = sums.pop((at, 1)).astype(BF16).T
                out_ref[1, 0, group, rows, :] = (
                    (sums.pop((at, 0)) * softmax_scale).astype(BF16).T
                )

    for item in range(len(items) + 2):
        for step, late in ((gather, 2), (score, 0), (weigh, 1)):
            if 0 <= item - late < len(items):
                step(item - late)
    dkv_ref[0, 0] = dkv_ref[0, 0] * softmax_scale


def finish(seen, kept, fetched, turned_q, turned_do, own_kv, near, lse, row_dot, softmax_scale):
    _, kv_count, own_groups, rows, width = kept.shape
    groups = 2 * own_groups
    own = pl.BlockSpec((1, 2, rows, width), lambda n: (n, 0, 0, 0))
    turned = pl.BlockSpec((1, width, groups * rows), lambda n: (n, 0, 0))
    stat = pl.BlockSpec((1, 8, groups * rows), lambda n: (n, 0, 0))
    half_groups = pl.BlockSpec((2, 1, own_groups, rows, width), lambda n: (0, n, 0, 0, 0))
    near_head = pl.BlockSpec((1,) + near.shape[1:], lambda n: (n, 0, 0, 0, 0, 0))
    return pl.pallas_call(
        functools.partial(finish_kernel, softmax_scale),
        grid=(kv_count,),
        out_shape=(
            jax.ShapeDtypeStruct(kept.shape, BF16),
            jax.ShapeDtypeStruct(kept.shape, BF16),
            jax.ShapeDtypeStruct(own_kv.shape, F32),
        ),
        in_specs=[
            pl.BlockSpec(memory_space=pltpu.SMEM),
            half_groups,
            half_groups,
            turned,
            turned,
            own,
            near_head,
            stat,
            stat,
        ],
        out_specs=(half_groups, half_groups, own),
        scratch_shapes=[pltpu.VMEM((2, 3, width, rows), BF16)],
        compiler_params=pltpu.CompilerParams(vmem_limit_bytes=GRANT),
        cost_estimate=pl.CostEstimate(
            flops=26 * kv_count * groups * rows * rows * width,
            bytes_accessed=16 * kv_count * groups * rows * width,
            transcendentals=3 * kv_count * groups * rows * rows,
        ),
        name="finish",
    )(seen, kept, fetched, turned_q, turned_do, own_kv, near, lse, row_dot)


def exchange(pieces):
    return lax.ppermute(pieces, "head", [(0, 1), (1, 0)])


def spread(pieces):
    return lax.all_to_all(pieces, "ctx", split_axis=0, concat_axis=0, tiled=True)


def on_device(queries, keys, values, output_gradient, selected):
    rows_block, own_groups, kv_count, width = queries.shape
    blocks = lax.axis_size("ctx")
    own_index = lax.axis_index("ctx")
    core = lax.axis_index("head")
    half_kv = kv_count // 2
    mine, theirs = core * half_kv, (1 - core) * half_kv
    softmax_scale = width ** (-0.5)
    piece_groups = blocks // (2 * half_kv)
    piece = rows_block // piece_groups
    picks = selected.reshape(-1)
    own_picks = lax.dynamic_index_in_dim(selected, own_index, 0, keepdims=False)
    seen = (own_picks < own_index).astype(jnp.int32)

    both = jnp.stack([keys, values], axis=0)
    both = lax.dynamic_slice_in_dim(both, mine, half_kv, axis=2)
    own_kv = jnp.transpose(both, (2, 0, 1, 3))
    inputs = jnp.transpose(jnp.stack([queries, output_gradient], axis=0), (0, 3, 2, 1, 4))
    kept = lax.dynamic_slice_in_dim(inputs, mine, half_kv, axis=1)
    fetched = exchange(lax.dynamic_slice_in_dim(inputs, theirs, half_kv, axis=1))

    held = spread(own_kv.reshape(blocks, piece, width))
    turned_q, turned_do, own_lse, own_dot = own_forward(kept, fetched, own_kv, softmax_scale)

    near = spread(pick_pieces(held, picks))
    near = near.reshape(half_kv, 2, piece_groups, 2, piece, width)
    lse, row_dot, dnear = near_attention(
        seen, turned_q, turned_do, near, own_lse, own_dot, softmax_scale, rows_block // 2
    )
    arrived = spread(dnear.reshape(blocks, 2 * piece, width))
    kept, moved, dkv = finish(
        seen, kept, fetched, turned_q, turned_do, own_kv, near, lse, row_dot, softmax_scale
    )
    home = spread(collect_pieces(arrived, picks))

    back = exchange(moved)
    whole = jnp.zeros((2, kv_count) + back.shape[2:], back.dtype)
    whole = lax.dynamic_update_slice_in_dim(whole, kept, mine, 1)
    whole = lax.dynamic_update_slice_in_dim(whole, back, theirs, 1)
    attn_out, grad_q = (jnp.transpose(whole[part], (2, 1, 0, 3)) for part in range(2))
    grads = (home.reshape(own_kv.shape).astype(F32) + dkv).astype(BF16)
    grad_k, grad_v = (jnp.transpose(grads[:, part], (1, 0, 2)) for part in range(2))
    return (attn_out, grad_q, grad_k, grad_v)


def solution(mesh):
    return jax.shard_map(
        on_device,
        mesh=mesh,
        in_specs=(
            P("ctx", "head", None, None),
            P("ctx", None, None),
            P("ctx", None, None),
            P("ctx", "head", None, None),
            P(),
        ),
        out_specs=(
            P("ctx", "head", None, None),
            P("ctx", "head", None, None),
            P("ctx", "head", None),
            P("ctx", "head", None),
        ),
        check_vma=False,
    )
```

```python
import functools
import math

import jax
import jax.numpy as jnp
from jax import lax
from jax.experimental import pallas as pl
from jax.experimental.pallas import tpu as pltpu
from jax.sharding import PartitionSpec as P

F32 = jnp.float32
BF16 = jnp.bfloat16
GRANT = 60 * 1024 * 1024
SMALL_GRANT = 8 * 1024 * 1024


def dot_nn(a, b):
    return lax.dot_general(a, b, (((1,), (0,)), ((), ())), preferred_element_type=F32)


def dot_nt(a, b):
    return lax.dot_general(a, b, (((1,), (1,)), ((), ())), preferred_element_type=F32)


def dot_tn(a, b):
    return lax.dot_general(a, b, (((0,), (0,)), ((), ())), preferred_element_type=F32)


def pick_kernel(picks, held, out):
    count, rows2, _ = out.shape
    rows = rows2 // 2
    first = pl.program_id(0) * count

    def body(step, _):
        for sub in range(8):
            at = step * 8 + sub
            for j in range(2):
                out[at, j * rows : (j + 1) * rows, :] = held[picks[(first + at) * 2 + j]]
        return 0

    lax.fori_loop(0, count // 8, body, 0)


def pick_pieces(held, picks):
    blocks, rows, width = held.shape
    steps = 2 if blocks % 16 == 0 else 1
    return pl.pallas_call(
        pick_kernel,
        grid=(steps,),
        out_shape=jax.ShapeDtypeStruct((blocks, 2 * rows, width), held.dtype),
        in_specs=[
            pl.BlockSpec(memory_space=pltpu.SMEM),
            pl.BlockSpec((blocks, rows, width), lambda i: (0, 0, 0)),
        ],
        out_specs=pl.BlockSpec((blocks // steps, 2 * rows, width), lambda i: (i, 0, 0)),
        compiler_params=pltpu.CompilerParams(vmem_limit_bytes=SMALL_GRANT),
        name="pick_pieces",
    )(picks, held)


def collect_kernel(picks, arrived, out, *totals):
    count, rows2, _ = arrived.shape
    rows = rows2 // 2
    part = pl.program_id(0)

    @pl.when(part == 0)
    def _():
        for total in totals:
            total[...] = jnp.zeros_like(total)

    def body(step, _):
        for sub in range(8):
            at = step * 8 + sub
            for j in range(2):
                owner = picks[(part * count + at) * 2 + j]
                totals[j][owner] += arrived[at, j * rows : (j + 1) * rows, :].astype(F32)
        return 0

    lax.fori_loop(0, count // 8, body, 0)

    @pl.when(part == pl.num_programs(0) - 1)
    def _():
        out[...] = (totals[0][...] + totals[1][...]).astype(out.dtype)


def collect_pieces(arrived, picks):
    blocks, rows2, width = arrived.shape
    steps = 2 if blocks % 16 == 0 else 1
    return pl.pallas_call(
        collect_kernel,
        grid=(steps,),
        out_shape=jax.ShapeDtypeStruct((blocks, rows2 // 2, width), arrived.dtype),
        in_specs=[
            pl.BlockSpec(memory_space=pltpu.SMEM),
            pl.BlockSpec((blocks // steps, rows2, width), lambda i: (i, 0, 0)),
        ],
        out_specs=pl.BlockSpec((blocks, rows2 // 2, width), lambda i: (0, 0, 0)),
        scratch_shapes=[pltpu.VMEM((blocks, rows2 // 2, width), F32)] * 2,
        compiler_params=pltpu.CompilerParams(vmem_limit_bytes=SMALL_GRANT),
        name="collect_pieces",
    )(picks, arrived)


def causal_pairs(rows):
    return lax.broadcasted_iota(jnp.int32, (rows, rows), 0) <= lax.broadcasted_iota(
        jnp.int32, (rows, rows), 1
    )


def own_forward_kernel(log_scale, q_ref, do_ref, kv_ref, qt_ref, dot_ref, lse_ref, row_dot_ref, vt):
    width = kv_ref.shape[3]
    half = kv_ref.shape[2] // 2
    seen = causal_pairs(half)

    @pl.when(pl.program_id(1) == 0)
    def _():
        vt[...] = kv_ref[0, 1].T

    turned_do = do_ref[0, 0].T
    qt_ref[0] = q_ref[0, 0].T
    dot_ref[0] = turned_do
    for tile in range(2):
        span = slice(tile * half, (tile + 1) * half)
        query = qt_ref[0, :, span]
        parts = []
        for col in range(tile + 1):
            scores = dot_nn(kv_ref[0, 0, col * half : (col + 1) * half, :], query)
            if col == tile:
                scores = jnp.where(seen, scores, -jnp.inf)
            parts.append(scores)
        top = parts[0].max(axis=0, keepdims=True)
        for scores in parts[1:]:
            top = jnp.maximum(top, scores.max(axis=0, keepdims=True))
        top = top * log_scale
        weight = jnp.zeros_like(top)
        total = jnp.zeros((width, half), F32)
        for col, scores in enumerate(parts):
            probs = jnp.exp2(scores * log_scale - top)
            weight = weight + probs.sum(axis=0, keepdims=True)
            total = total + dot_nn(vt[:, col * half : (col + 1) * half], probs.astype(BF16))
        row_dot = jnp.sum(total * turned_do[:, span].astype(F32), axis=0, keepdims=True) / weight
        lse_ref[0, :, span] = jnp.broadcast_to(top + jnp.log2(weight), (8, half))
        row_dot_ref[0, :, span] = jnp.broadcast_to(row_dot, (8, half))


def own_forward(queries, grads, own_kv, softmax_scale):
    kv_count, groups, rows, width = queries.shape
    by_group = pl.BlockSpec((1, 1, rows, width), lambda n, g: (n, g, 0, 0))
    turned = pl.BlockSpec((1, width, rows), lambda n, g: (n, 0, g))
    stat = pl.BlockSpec((1, 8, rows), lambda n, g: (n, 0, g))
    return pl.pallas_call(
        functools.partial(own_forward_kernel, softmax_scale * math.log2(math.e)),
        grid=(kv_count, groups),
        out_shape=(
            jax.ShapeDtypeStruct((kv_count, width, groups * rows), BF16),
            jax.ShapeDtypeStruct((kv_count, width, groups * rows), BF16),
            jax.ShapeDtypeStruct((kv_count, 8, groups * rows), F32),
            jax.ShapeDtypeStruct((kv_count, 8, groups * rows), F32),
        ),
        in_specs=[
            by_group,
            by_group,
            pl.BlockSpec((1, 2, rows, width), lambda n, g: (n, 0, 0, 0)),
        ],
        out_specs=(turned, turned, stat, stat),
        scratch_shapes=[pltpu.VMEM((width, rows), BF16)],
        compiler_params=pltpu.CompilerParams(vmem_limit_bytes=GRANT),
        cost_estimate=pl.CostEstimate(
            flops=4 * kv_count * groups * rows * rows * width,
            bytes_accessed=12 * kv_count * groups * rows * width,
            transcendentals=kv_count * groups * rows * rows,
        ),
        name="own_forward",
    )(queries, grads, own_kv)


def near_kernel(
    softmax_scale,
    tile,
    seen_ref,
    qt_ref,
    dot_ref,
    near_ref,
    own_lse_ref,
    own_dot_ref,
    lse_ref,
    row_dot_ref,
    dnear_ref,
    dk_acc,
    dv_acc,
):
    log_scale = softmax_scale * math.log2(math.e)
    groups, _, piece, width = near_ref.shape[2:]
    rows = groups * piece
    seen = [seen_ref[j] > 0 for j in range(2)]
    count = qt_ref.shape[2] // tile
    held = [{} for _ in range(count)]
    dk_acc[...] = jnp.zeros_like(dk_acc)
    dv_acc[...] = jnp.zeros_like(dv_acc)

    def span(at):
        return slice(at * tile, (at + 1) * tile)

    def score(at, j):
        scores = dot_nn(near_ref[0, 0, :, j].reshape(rows, width), qt_ref[0, :, span(at)])
        held[at]["scores", j] = scores
        held[at]["peak", j] = scores.max(axis=0, keepdims=True) * log_scale

    def settle(at):
        own_lse = own_lse_ref[0, :1, span(at)]
        top = own_lse
        for j in range(2):
            top = jnp.maximum(top, jnp.where(seen[j], held[at].pop(("peak", j)), -jnp.inf))
        share = jnp.exp2(own_lse - top)
        held[at]["top"] = top
        held[at]["weight"] = share
        held[at]["dot"] = share * own_dot_ref[0, :1, span(at)]

    def weigh(at, j):
        grad_probs = dot_nn(near_ref[0, 1, :, j].reshape(rows, width), dot_ref[0, :, span(at)])
        shift = jnp.where(seen[j], held[at]["top"], jnp.inf)
        probs = jnp.exp2(held[at].pop(("scores", j)) * log_scale - shift)
        held[at]["weight"] += probs.sum(axis=0, keepdims=True)
        held[at]["dot"] += (probs * grad_probs).sum(axis=0, keepdims=True)
        held[at]["low", j] = probs.astype(BF16)
        held[at]["grad_probs", j] = grad_probs

    def normalise(at):
        weight = held[at]["weight"]
        inverse = 1.0 / weight
        row_dot = held[at]["dot"] * inverse
        held[at]["row_dot"] = row_dot
        lse = held[at]["top"] + jnp.log2(weight)
        lse_ref[0, :, span(at)] = jnp.broadcast_to(lse, (8, tile))
        row_dot_ref[0, :, span(at)] = jnp.broadcast_to(row_dot, (8, tile))
        held[at]["grads"] = (dot_ref[0, :, span(at)].astype(F32) * inverse).astype(BF16).T
        held[at]["query"] = (qt_ref[0, :, span(at)].astype(F32) * inverse).astype(BF16).T

    def differ(at, j):
        change = held[at].pop(("grad_probs", j)) - held[at]["row_dot"]
        held[at]["grad_scores", j] = held[at]["low", j] * change.astype(BF16)

    def gather(at, j):
        dv_acc[j] += dot_nn(held[at].pop(("low", j)), held[at]["grads"])
        dk_acc[j] += dot_nn(held[at].pop(("grad_scores", j)), held[at]["query"])

    def stage(step, at, *parts):
        if 0 <= at < count:
            step(at, *parts)

    for at in range(count + 3):
        stage(settle, at - 1)
        stage(normalise, at - 2)
        for j in range(2):
            stage(gather, at - 3, j)
            stage(score, at, j)
            stage(weigh, at - 1, j)
            stage(differ, at - 2, j)

    for j in range(2):
        dnear_ref[0, 0, :, j] = (
            (dk_acc[j] * softmax_scale).astype(BF16).reshape(groups, piece, width)
        )
        dnear_ref[0, 1, :, j] = dv_acc[j].astype(BF16).reshape(groups, piece, width)


def near_attention(seen, turned_q, turned_do, near, own_lse, own_dot, softmax_scale, tile):
    kv_count, width, rows = turned_q.shape
    _, _, groups, _, piece, _ = near.shape
    key_rows = groups * piece
    turned = pl.BlockSpec((1, width, rows), lambda n: (n, 0, 0))
    stat = pl.BlockSpec((1, 8, rows), lambda n: (n, 0, 0))
    by_head = pl.BlockSpec((1,) + near.shape[1:], lambda n: (n, 0, 0, 0, 0, 0))
    return pl.pallas_call(
        functools.partial(near_kernel, softmax_scale, tile),
        grid=(kv_count,),
        out_shape=(
            jax.ShapeDtypeStruct((kv_count, 8, rows), F32),
            jax.ShapeDtypeStruct((kv_count, 8, rows), F32),
            jax.ShapeDtypeStruct(near.shape, BF16),
        ),
        in_specs=[pl.BlockSpec(memory_space=pltpu.SMEM), turned, turned, by_head, stat, stat],
        out_specs=(stat, stat, by_head),
        scratch_shapes=[
            pltpu.VMEM((2, key_rows, width), F32),
            pltpu.VMEM((2, key_rows, width), F32),
        ],
        compiler_params=pltpu.CompilerParams(vmem_limit_bytes=GRANT),
        cost_estimate=pl.CostEstimate(
            flops=16 * kv_count * rows * key_rows * width,
            bytes_accessed=10 * kv_count * rows * width,
            transcendentals=2 * kv_count * rows * key_rows,
        ),
        name="near_attention",
    )(seen, turned_q, turned_do, near, own_lse, own_dot)


def finish_kernel(
    softmax_scale,
    seen_ref,
    q_ref,
    do_ref,
    qt_ref,
    dot_ref,
    kv_ref,
    near_ref,
    lse_ref,
    row_dot_ref,
    kept_ref,
    moved_ref,
    dkv_ref,
    turned_kv,
):
    log_scale = softmax_scale * math.log2(math.e)
    group_count, block = q_ref.shape[1:3]
    groups, _, piece, width = near_ref.shape[2:]
    tile = block // 2
    triangle = causal_pairs(tile)
    dkv_ref[...] = jnp.zeros_like(dkv_ref)
    for kind in range(2):
        for j in range(2):
            turned_kv[kind, j] = near_ref[0, kind, :, j].reshape(block, width).T
        turned_kv[kind, 2] = kv_ref[0, kind].T
    items = []
    for at in range(group_count * 2):
        own = [(at, 2, col) for col in range(at % 2 + 1)]
        items += [(at, 0, None), (at, 1, None)] + own
    held = [{} for _ in items]
    sums = {}

    def keys_of(kind, j, col):
        if j < 2:
            return near_ref[0, kind, :, j].reshape(block, width)
        return kv_ref[0, kind, col * tile : (col + 1) * tile, :]

    def turned_of(kind, j, col):
        if j < 2:
            return turned_kv[kind, j]
        return turned_kv[kind, 2, :, col * tile : (col + 1) * tile]

    def score(item):
        at, j, col = items[item]
        held[item]["scores"] = dot_nn(keys_of(0, j, col), qt_ref[0, :, at * tile : (at + 1) * tile])

    def weigh(item):
        at, j, col = items[item]
        span = slice(at * tile, (at + 1) * tile)
        grad_probs = dot_nn(keys_of(1, j, col), dot_ref[0, :, span])
        lse = lse_ref[0, :1, span]
        if j < 2:
            lse = jnp.where(seen_ref[j] > 0, lse, jnp.inf)
        probs = jnp.exp2(held[item].pop("scores") * log_scale - lse)
        if j == 2 and col == at % 2:
            probs = jnp.where(triangle, probs, 0.0)
        held[item]["low"] = probs.astype(BF16)
        held[item]["grad_scores"] = (probs * (grad_probs - row_dot_ref[0, :1, span])).astype(BF16)

    def gather(item):
        at, j, col = items[item]
        low, grad_scores = held[item].pop("low"), held[item].pop("grad_scores")
        for kind, factor in ((1, low), (0, grad_scores)):
            term = dot_nn(turned_of(kind, j, col), factor)
            sums[at, kind] = sums[at, kind] + term if (at, kind) in sums else term
        group, rows = at // 2, slice(at % 2 * tile, (at % 2 + 1) * tile)
        if j == 2:
            cols = slice(col * tile, (col + 1) * tile)
            dkv_ref[0, 0, cols, :] += dot_nn(grad_scores, q_ref[0, group, rows, :])
            dkv_ref[0, 1, cols, :] += dot_nn(low, do_ref[0, group, rows, :])
            if col == at % 2:
                out_ref = kept_ref if 2 * group < group_count else moved_ref
                group = group % (group_count // 2)
                out_ref[0, 0, group, rows, :] = sums.pop((at, 1)).astype(BF16).T
                out_ref[1, 0, group, rows, :] = (
                    (sums.pop((at, 0)) * softmax_scale).astype(BF16).T
                )

    for item in range(len(items) + 2):
        for step, late in ((gather, 2), (score, 0), (weigh, 1)):
            if 0 <= item - late < len(items):
                step(item - late)
    dkv_ref[0, 0] = dkv_ref[0, 0] * softmax_scale


def finish(seen, queries, grads, turned_q, turned_do, own_kv, near, lse, row_dot, softmax_scale):
    kv_count, groups, rows, width = queries.shape
    by_head = pl.BlockSpec((1, groups, rows, width), lambda n: (n, 0, 0, 0))
    own = pl.BlockSpec((1, 2, rows, width), lambda n: (n, 0, 0, 0))
    turned = pl.BlockSpec((1, width, groups * rows), lambda n: (n, 0, 0))
    stat = pl.BlockSpec((1, 8, groups * rows), lambda n: (n, 0, 0))
    half_groups = pl.BlockSpec((2, 1, groups // 2, rows, width), lambda n: (0, n, 0, 0, 0))
    near_head = pl.BlockSpec((1,) + near.shape[1:], lambda n: (n, 0, 0, 0, 0, 0))
    return pl.pallas_call(
        functools.partial(finish_kernel, softmax_scale),
        grid=(kv_count,),
        out_shape=(
            jax.ShapeDtypeStruct((2, kv_count, groups // 2, rows, width), BF16),
            jax.ShapeDtypeStruct((2, kv_count, groups // 2, rows, width), BF16),
            jax.ShapeDtypeStruct(own_kv.shape, F32),
        ),
        in_specs=[
            pl.BlockSpec(memory_space=pltpu.SMEM),
            by_head,
            by_head,
            turned,
            turned,
            own,
            near_head,
            stat,
            stat,
        ],
        out_specs=(half_groups, half_groups, own),
        scratch_shapes=[pltpu.VMEM((2, 3, width, rows), BF16)],
        compiler_params=pltpu.CompilerParams(vmem_limit_bytes=GRANT),
        cost_estimate=pl.CostEstimate(
            flops=26 * kv_count * groups * rows * rows * width,
            bytes_accessed=16 * kv_count * groups * rows * width,
            transcendentals=3 * kv_count * groups * rows * rows,
        ),
        name="finish",
    )(seen, queries, grads, turned_q, turned_do, own_kv, near, lse, row_dot)


def exchange(pieces):
    return lax.ppermute(pieces, "head", [(0, 1), (1, 0)])


def spread(pieces):
    return lax.all_to_all(pieces, "ctx", split_axis=0, concat_axis=0, tiled=True)


def on_device(queries, keys, values, output_gradient, selected):
    rows_block, own_groups, kv_count, width = queries.shape
    blocks = lax.axis_size("ctx")
    own_index = lax.axis_index("ctx")
    core = lax.axis_index("head")
    half_kv = kv_count // 2
    mine, theirs = core * half_kv, (1 - core) * half_kv
    softmax_scale = width ** (-0.5)
    piece_groups = blocks // (2 * half_kv)
    piece = rows_block // piece_groups
    picks = selected.reshape(-1)
    own_picks = lax.dynamic_index_in_dim(selected, own_index, 0, keepdims=False)
    seen = (own_picks < own_index).astype(jnp.int32)

    both = jnp.stack([keys, values], axis=0)
    both = lax.dynamic_slice_in_dim(both, mine, half_kv, axis=2)
    own_kv = jnp.transpose(both, (2, 0, 1, 3))
    held = spread(own_kv.reshape(blocks, piece, width))

    inputs = jnp.transpose(jnp.stack([queries, output_gradient], axis=0), (0, 3, 2, 1, 4))
    kept = lax.dynamic_slice_in_dim(inputs, mine, half_kv, axis=1)
    fetched = exchange(lax.dynamic_slice_in_dim(inputs, theirs, half_kv, axis=1))
    inputs = jnp.concatenate([kept, fetched], axis=2)
    q_all, do_all = inputs[0], inputs[1]
    turned_q, turned_do, own_lse, own_dot = own_forward(q_all, do_all, own_kv, softmax_scale)

    near = spread(pick_pieces(held, picks))
    near = near.reshape(half_kv, 2, piece_groups, 2, piece, width)
    lse, row_dot, dnear = near_attention(
        seen, turned_q, turned_do, near, own_lse, own_dot, softmax_scale, rows_block // 2
    )
    arrived = spread(dnear.reshape(blocks, 2 * piece, width))
    kept, moved, dkv = finish(
        seen, q_all, do_all, turned_q, turned_do, own_kv, near, lse, row_dot, softmax_scale
    )
    home = spread(collect_pieces(arrived, picks))

    back = exchange(moved)
    whole = jnp.zeros((2, kv_count) + back.shape[2:], back.dtype)
    whole = lax.dynamic_update_slice_in_dim(whole, kept, mine, 1)
    whole = lax.dynamic_update_slice_in_dim(whole, back, theirs, 1)
    attn_out, grad_q = (jnp.transpose(whole[part], (2, 1, 0, 3)) for part in range(2))
    home = home.reshape(own_kv.shape)
    grad_k, grad_v = (
        (
            jnp.stack([home[n, part] for n in range(half_kv)], axis=1).astype(F32)
            + jnp.stack([dkv[n, part] for n in range(half_kv)], axis=1)
        ).astype(BF16)
        for part in range(2)
    )
    return (attn_out, grad_q, grad_k, grad_v)


def solution(mesh):
    return jax.shard_map(
        on_device,
        mesh=mesh,
        in_specs=(
            P("ctx", "head", None, None),
            P("ctx", None, None),
            P("ctx", None, None),
            P("ctx", "head", None, None),
            P(),
        ),
        out_specs=(
            P("ctx", "head", None, None),
            P("ctx", "head", None, None),
            P("ctx", "head", None),
            P("ctx", "head", None),
        ),
        check_vma=False,
    )
```
